128 devices in a mesh: lat: 8 (over z_lo, x), lon: 16 (over y, z_hi, core).
Axes of the slice: x: 4, y: 4, z: 4 (z_hi: 2, z_lo: 2; z = z_hi * 2 + z_lo), core: 2. Of those that a mesh axis runs over, the one named last changes fastest.
Arguments:
- grid_state: bfloat16 [64, 256, 512], P('lat', 'lon'), may hold values from -6 to 6
- observations: bfloat16 [32768, 256], P(('lat', 'lon')), may hold values from -6 to 6
- target_tile: int32 [32768, 1], P(('lat', 'lon')), may hold values from 0 to 127; in each aligned block of 256 rows (0 to 255, 256 to 511, ...) at most 6 rows name the same one
- target_cell: int32 [32768], P(('lat', 'lon')), may hold values from 0 to 127
- accepted: int32 [32768], P(('lat', 'lon')), may hold values 0 or 1
- query_weight: bfloat16 [512, 512], replicated, may hold values from -0.25 to 0.25
- sensor_weight: bfloat16 [256, 1024], replicated, may hold values from -0.375 to 0.375
- cross_weight: bfloat16 [512, 512], replicated, may hold values from -0.25 to 0.25
- local_weight: bfloat16 [512, 1536], replicated, may hold values from -0.25 to 0.25
- merge_weight: bfloat16 [512, 512], replicated, may hold values from -0.25 to 0.25
- cotangent: bfloat16 [64, 256, 512], P('lat', 'lon'), may hold values from -6 to 6
Outputs:
- updated: bfloat16 [64, 256, 512], P('lat', 'lon')
- grad_grid: float32 [64, 256, 512], P('lat', 'lon')
- grad_observations: bfloat16 [32768, 256], P(('lat', 'lon'))
- grad_query_weight: float32 [512, 512], replicated
- grad_sensor_weight: float32 [256, 1024], replicated
- grad_cross_weight: float32 [512, 512], replicated
- grad_local_weight: float32 [512, 1536], replicated
- grad_merge_weight: float32 [512, 512], replicated
The draws below stay inside these ranges and needn't reach their ends.
Inputs may be any that keep to these rules, and one draw needn't show every extreme that they name: `target_tile`: within the rows of one device no tile is named by more than 6 rows, a bound that some block reaches.
All inputs are finite; a program needn't handle non-finite values. No bound on the sum of `accepted` on one device may be relied on, other than what follows from the above.
Results may differ from the reference program's by a relative error of at most 0.023.
The reference program's roundings to bfloat16 on the way count: a program that leaves them out, or rounds other values in their place, can miss the bound.
Values may be sent and summed in bfloat16 or wider, within the bound.
No kernel may reach another device: no remote copies, remote signals or barrier semaphores. Data moves between devices by JAX's collectives and lax.ppermute only.
A program may use at most 128 MiB of HBM per device.

```python
import math
import jax
import jax.numpy as jnp
import numpy as np
from jax import lax

C = 512
HEADS = 16
F = 256
RADIUS = 6
TH = 8
TW = 16
OBS_DEV = 256
CAP = 6
SLOTS = 768
NLAT = 64
NLON = 256
OBS = 32768
N_LAT = 8
N_LON = 16
DEVICES = 128


def draw_grid_state(key, part):
    key = jax.random.fold_in(key, 11)
    return jnp.clip(jax.random.normal(key, (NLAT, NLON, C), jnp.float32), -6.0, 6.0).astype(jnp.bfloat16)


def draw_observations(key, part):
    key = jax.random.fold_in(key, 12)
    return jnp.clip(jax.random.normal(key, (OBS, F), jnp.float32), -6.0, 6.0).astype(jnp.bfloat16)


def place_ends(array, stream_key, smallest, top_value):
    longest = array.shape.index(max(array.shape))
    spots = []
    for shift in (0, 1):
        where = [jax.random.randint(jax.random.fold_in(stream_key, axis), (), 0, length) for axis, length in enumerate(array.shape)]
        where[longest] = (where[longest] + shift) % array.shape[longest]
        spots.append(tuple(where))
    return array.at[spots[0]].set(smallest).at[spots[1]].set(top_value)


def levels(stream_key, dims, pieces, smallest, top_value):
    def one(position, parts):
        steps = jax.random.uniform(jax.random.fold_in(jax.random.fold_in(stream_key, 6), position), (parts,), jnp.float32, smallest / len(pieces), top_value / len(pieces))
        return jnp.repeat(jnp.exp(steps), dims[position] // parts).reshape((-1,) + (1,) * (len(dims) - position - 1))

    loudness = one(*pieces[0])
    for cut in pieces[1:]:
        loudness = loudness * one(*cut)
    return loudness


def routed_block(key, own, number, rows, amount, top, reach, skew):
    ranking = jax.random.permutation(key, amount)
    heavy_load, ordinary = portions_of(amount, rows * top, reach, skew, True), portions_of(amount, rows * top, reach, skew, False)
    places = jnp.arange(amount)

    def named(sizes, offset_by):
        used = int((sizes > 0).sum())
        fixed = max(1, used // 4)
        shifted = fixed + (places - fixed + offset_by * (used - fixed)) % max(1, amount - fixed)
        return jnp.zeros((amount,), jnp.int32).at[ranking[jnp.where(places < fixed, places, shifted)]].set(jnp.asarray(sizes, jnp.int32))

    sizes = jnp.where(number % 4 == 0, named(heavy_load, number // 4), named(ordinary, number - number // 4 - 1))
    mixed = jax.random.permutation(jax.random.fold_in(own, 3), amount)
    giver, taker = mixed[0:amount // 2 * 2:2], mixed[1:amount // 2 * 2:2]
    slack = jnp.minimum(sizes[giver] - 1, reach - sizes[taker]) // 2
    slack = jnp.where((giver == ranking[0]) | (taker == ranking[0]) | (sizes[taker] == 0), 0, jnp.maximum(slack, 0))
    shifted = jax.random.randint(jax.random.fold_in(own, 4), (amount // 2,), 0, 1 << 20) % (slack + 1)
    sizes = sizes.at[giver].add(-shifted).at[taker].add(shifted)
    items = jnp.searchsorted(jnp.cumsum(sizes), jnp.arange(rows * top), side="right").astype(jnp.int32)
    listing = items.reshape(top, rows).T
    listing = listing[jax.random.permutation(jax.random.fold_in(own, 1), rows)]
    offset_by = jax.random.randint(jax.random.fold_in(own, 2), (rows, 1), 0, top)
    return jnp.take_along_axis(listing, (jnp.arange(top)[None, :] + offset_by) % top, axis=1)


def portions_of(amount, total, reach, slope, full):
    weights = [(1 << 20) // math.isqrt(grade ** slope) + 1 for grade in range(1, amount + 1)]
    largest = reach if full else min(reach, max(-(-total // amount), total * weights[0] // sum(weights)))
    least = 1 if total - largest >= amount - 1 else 0
    holding, surplus = [largest] + [least] * (amount - 1), total - largest - least * (amount - 1)
    while surplus > 0:
        free = [i for i in range(1, amount) if holding[i] < largest] or [i for i in range(1, amount) if holding[i] < reach]
        whole, budget = sum([weights[i] for i in free]), surplus
        for i in free:
            more = min(reach - holding[i], max(1, budget * weights[i] // whole), surplus)
            holding[i] = holding[i] + more
            surplus = surplus - more
    return np.array(holding)


def centred(stream_key, dims, width, most, pieces=(), kind=jnp.bfloat16):
    result = width * jax.random.normal(stream_key, dims, jnp.float32)
    if pieces:
        result = result * levels(stream_key, dims, pieces, -0.22, 0.18)
    return jnp.clip(result, -most, most).astype(kind)


def setup_inputs(seed: int = 0) -> dict:
    splits = jax.random.split(jax.random.key(seed), 12)
    grid_state = draw_grid_state(jax.random.fold_in(splits[11], 71), 0)
    observations = draw_observations(jax.random.fold_in(splits[11], 71), 0)
    target_tile_keys = jax.random.split(jax.random.fold_in(splits[2], 1), OBS // OBS_DEV)
    target_tile_turns = jax.random.permutation(jax.random.fold_in(splits[2], 3), OBS // OBS_DEV)
    target_tile = jax.vmap(lambda own, number: routed_block(jax.random.fold_in(splits[2], 2), own, number, OBS_DEV, DEVICES, 1, CAP, 2))(target_tile_keys, target_tile_turns).reshape((OBS, 1))
    target_cell = place_ends(jax.random.randint(splits[3], (OBS,), 0, TH * TW), jax.random.fold_in(splits[3], 1), 0, (TH * TW) - 1).astype(jnp.int32)
    accepted = place_ends((jax.random.randint(splits[4], (OBS,), 0, 4) < 3).astype(jnp.int32), jax.random.fold_in(splits[4], 1), 0, 1)
    query_weight = centred(splits[5], (C, C), C ** -0.5, 0.25)
    sensor_weight = centred(splits[6], (F, 2 * C), F ** -0.5, 0.375)
    cross_weight = centred(splits[7], (C, C), C ** -0.5, 0.25)
    local_weight = centred(splits[8], (C, 3 * C), C ** -0.5, 0.25)
    merge_weight = centred(splits[9], (C, C), C ** -0.5, 0.25)
    cotangent = centred(splits[10], (NLAT, NLON, C), 1.0, 6.0, ((0, 8), (1, 16)))
    return dict(grid_state=grid_state, observations=observations, target_tile=target_tile, target_cell=target_cell, accepted=accepted, query_weight=query_weight, sensor_weight=sensor_weight, cross_weight=cross_weight, local_weight=local_weight, merge_weight=merge_weight, cotangent=cotangent)


def head_cols(matrix, head, head_width):
    return lax.dynamic_slice_in_dim(matrix, head * head_width, head_width, 1)

def joined(stacked):
    head_count, row_count, head_width = stacked.shape
    return jnp.transpose(stacked, (1, 0, 2)).reshape(row_count, head_count * head_width)

def head_bias(head, head_count, tile_rows, tile_cols, row_code, col_code):
    cell_index = jnp.arange(tile_rows * tile_cols, dtype=jnp.int32)
    query_row = (cell_index // tile_cols).astype(jnp.float32)
    query_col = (cell_index % tile_cols).astype(jnp.float32)
    bias_slope = 8.0 * jnp.exp2(-8.0 * head.astype(jnp.float32) / head_count)
    row_gap = (query_row[:, None] - (row_code[None, :] - 1.0)) / tile_rows
    col_gap = (query_col[:, None] - col_code[None, :]) / tile_cols
    return -bias_slope * (row_gap * row_gap + col_gap * col_gap)

def cross_scores(head, queries, key_rows, row_code, col_code, tile_rows, tile_cols, head_count):
    head_width = queries.shape[1] // head_count
    scores = jnp.dot(head_cols(queries, head, head_width), head_cols(key_rows, head, head_width).T, preferred_element_type=jnp.float32) / math.sqrt(head_width)
    scores = scores + head_bias(head, head_count, tile_rows, tile_cols, row_code, col_code)
    return jnp.where(row_code[None, :] > 0.5, scores, -1e+30)

def cross_forward(queries, keyval, row_code, col_code, tile_rows, tile_cols, head_count):
    channels = queries.shape[1]
    head_width = channels // head_count
    key_rows = keyval[:, :channels]
    values = keyval[:, channels:]

    def one_head(head):
        scores = cross_scores(head, queries, key_rows, row_code, col_code, tile_rows, tile_cols, head_count)
        row_max = jnp.maximum(lax.optimization_barrier(jnp.max(scores, axis=1)), 0.0)
        row_total = jnp.exp(-row_max) + lax.optimization_barrier(jnp.sum(jnp.exp(scores - row_max[:, None]), axis=1))
        log_total = row_max + jnp.log(row_total)
        probability = jnp.exp(scores - log_total[:, None]).astype(jnp.bfloat16)
        return (jnp.dot(probability, head_cols(values, head, head_width), preferred_element_type=jnp.float32), log_total)
    blended, log_total = lax.map(one_head, jnp.arange(head_count, dtype=jnp.int32))
    return (joined(blended).astype(jnp.bfloat16), log_total)

def cross_backward(queries, keyval, row_code, col_code, log_total, grad_att, tile_rows, tile_cols, head_count):
    channels = queries.shape[1]
    head_width = channels // head_count
    key_rows = keyval[:, :channels]
    values = keyval[:, channels:]

    def one_head(inputs):
        head, head_total = inputs
        scores = cross_scores(head, queries, key_rows, row_code, col_code, tile_rows, tile_cols, head_count)
        probability = jnp.exp(scores - head_total[:, None])
        head_grad = head_cols(grad_att, head, head_width)
        grad_prob = jnp.dot(head_grad, head_cols(values, head, head_width).T, preferred_element_type=jnp.float32)
        row_delta = lax.optimization_barrier(jnp.sum(probability * grad_prob, axis=1))
        grad_score = (probability * (grad_prob - row_delta[:, None])).astype(jnp.bfloat16)
        grad_query = jnp.dot(grad_score, head_cols(key_rows, head, head_width), preferred_element_type=jnp.float32) / math.sqrt(head_width)
        grad_key = jnp.dot(grad_score.T, head_cols(queries, head, head_width), preferred_element_type=jnp.float32) / math.sqrt(head_width)
        grad_value = jnp.dot(probability.astype(jnp.bfloat16).T, head_grad, preferred_element_type=jnp.float32)
        return (grad_query, grad_key, grad_value)
    grad_query, grad_key, grad_value = lax.map(one_head, (jnp.arange(head_count, dtype=jnp.int32), log_total))
    grad_keyval = jnp.concatenate([joined(grad_key), joined(grad_value)], axis=1).astype(jnp.bfloat16)
    return (joined(grad_query).astype(jnp.bfloat16), grad_keyval)

def make_window(lat_index, lat_count, tile_rows, tile_cols):
    wide_cols = tile_cols + 2 * RADIUS
    cell_index = jnp.arange(tile_rows * tile_cols, dtype=jnp.int32)
    query_row = cell_index // tile_cols
    query_col = cell_index % tile_cols
    key_index = jnp.arange((tile_rows + 2 * RADIUS) * wide_cols, dtype=jnp.int32)
    key_row = key_index // wide_cols
    key_col = key_index % wide_cols
    nearby = (jnp.abs(key_row[None, :] - RADIUS - query_row[:, None]) <= RADIUS) & (jnp.abs(key_col[None, :] - RADIUS - query_col[:, None]) <= RADIUS)
    global_row = lat_index * tile_rows + key_row - RADIUS
    inside = (global_row >= 0) & (global_row < lat_count * tile_rows)
    return nearby & inside[None, :]

def local_forward(queries, padded_kv, allowed, head_count):
    channels = queries.shape[1]
    head_width = channels // head_count
    key_rows = padded_kv[:, :channels]
    values = padded_kv[:, channels:]

    def one_head(head):
        scores = jnp.dot(head_cols(queries, head, head_width), head_cols(key_rows, head, head_width).T, preferred_element_type=jnp.float32) / math.sqrt(head_width)
        scores = jnp.where(allowed, scores, -1e+30)
        row_max = lax.optimization_barrier(jnp.max(scores, axis=1))
        log_total = row_max + jnp.log(lax.optimization_barrier(jnp.sum(jnp.exp(scores - row_max[:, None]), axis=1)))
        probability = jnp.exp(scores - log_total[:, None]).astype(jnp.bfloat16)
        return (jnp.dot(probability, head_cols(values, head, head_width), preferred_element_type=jnp.float32), log_total)
    blended, log_total = lax.map(one_head, jnp.arange(head_count, dtype=jnp.int32))
    return (joined(blended).astype(jnp.bfloat16), log_total)

def local_back_queries(queries, padded_kv, allowed, log_total, grad_att, head_count):
    channels = queries.shape[1]
    head_width = channels // head_count
    key_rows = padded_kv[:, :channels]
    values = padded_kv[:, channels:]

    def one_head(inputs):
        head, head_total = inputs
        head_key = head_cols(key_rows, head, head_width)
        scores = jnp.dot(head_cols(queries, head, head_width), head_key.T, preferred_element_type=jnp.float32) / math.sqrt(head_width)
        scores = jnp.where(allowed, scores, -1e+30)
        probability = jnp.exp(scores - head_total[:, None])
        grad_prob = jnp.dot(head_cols(grad_att, head, head_width), head_cols(values, head, head_width).T, preferred_element_type=jnp.float32)
        row_delta = lax.optimization_barrier(jnp.sum(probability * grad_prob, axis=1))
        grad_score = (probability * (grad_prob - row_delta[:, None])).astype(jnp.bfloat16)
        return (jnp.dot(grad_score, head_key, preferred_element_type=jnp.float32) / math.sqrt(head_width), row_delta)
    grad_query, row_delta = lax.map(one_head, (jnp.arange(head_count, dtype=jnp.int32), log_total))
    return (joined(grad_query), row_delta)

def local_back_keys(keyval, padded_query, padded_grad, padded_total, padded_delta, allowed, head_count):
    channels = keyval.shape[1] // 2
    head_width = channels // head_count
    key_rows = keyval[:, :channels]
    values = keyval[:, channels:]

    def one_head(inputs):
        head, head_total, head_delta = inputs
        head_query = head_cols(padded_query, head, head_width)
        head_grad = head_cols(padded_grad, head, head_width)
        scores = jnp.dot(head_cols(key_rows, head, head_width), head_query.T, preferred_element_type=jnp.float32) / math.sqrt(head_width)
        scores = jnp.where(allowed, scores, -1e+30)
        probability = jnp.exp(scores - head_total[None, :])
        grad_prob = jnp.dot(head_cols(values, head, head_width), head_grad.T, preferred_element_type=jnp.float32)
        grad_score = (probability * (grad_prob - head_delta[None, :])).astype(jnp.bfloat16)
        grad_key = jnp.dot(grad_score, head_query, preferred_element_type=jnp.float32) / math.sqrt(head_width)
        grad_value = jnp.dot(probability.astype(jnp.bfloat16), head_grad, preferred_element_type=jnp.float32)
        return (grad_key, grad_value)
    grad_key, grad_value = lax.map(one_head, (jnp.arange(head_count, dtype=jnp.int32), padded_total, padded_delta))
    return (joined(grad_key), joined(grad_value))

def pad_rim(field):
    wrapped = jnp.concatenate([field[:, -RADIUS:], field, field[:, :RADIUS]], axis=1)
    return jnp.pad(wrapped, ((RADIUS, RADIUS), (0, 0), (0, 0)))

def to_tiles(field):
    channels = field.shape[-1]
    shaped = field.reshape(N_LAT, TH, N_LON, TW, channels).transpose(0, 2, 1, 3, 4)
    return shaped.reshape(N_LAT * N_LON, TH * TW, channels)

def from_tiles(tiles):
    channels = tiles.shape[-1]
    shaped = tiles.reshape(N_LAT, N_LON, TH, TW, channels).transpose(0, 2, 1, 3, 4)
    return shaped.reshape(N_LAT * TH, N_LON * TW, channels)

def rim_tile(padded, tile):
    channels = padded.shape[-1]
    band = tile // N_LON
    sector = tile % N_LON
    window_block = lax.dynamic_slice(padded, (band * TH, sector * TW, band * 0), (TH + 2 * RADIUS, TW + 2 * RADIUS, channels))
    return window_block.reshape(-1, channels)

def reference(grid_state, observations, target_tile, target_cell, accepted, query_weight, sensor_weight, cross_weight, local_weight, merge_weight, cotangent):
    tile_count = N_LAT * N_LON
    channels = grid_state.shape[2]
    cell_count = TH * TW
    tile_ids = jnp.arange(tile_count, dtype=jnp.int32)
    destination = target_tile[:, 0]
    dest_hits = (destination[:, None] == tile_ids[None, :]).astype(jnp.int32).reshape(tile_count, OBS_DEV, tile_count)
    earlier = jnp.cumsum(dest_hits, axis=1, dtype=jnp.int32) - dest_hits
    slot_rank = lax.optimization_barrier(jnp.sum(earlier * dest_hits, axis=2, dtype=jnp.int32)).reshape(-1)
    source = jnp.arange(OBS, dtype=jnp.int32) // OBS_DEV
    where_to = (destination * SLOTS + source * CAP + slot_rank).astype(jnp.int32)
    received = jnp.zeros((tile_count * SLOTS, F), observations.dtype).at[where_to].set(observations)
    received = received.reshape(tile_count, SLOTS, F)
    row_code = jnp.zeros((tile_count * SLOTS,), jnp.float32).at[where_to].set(((target_cell // TW + 1) * accepted).astype(jnp.float32)).reshape(tile_count, SLOTS)
    col_code = jnp.zeros((tile_count * SLOTS,), jnp.float32).at[where_to].set((target_cell % TW).astype(jnp.float32)).reshape(tile_count, SLOTS)
    grid_rows = to_tiles(grid_state).reshape(-1, channels)
    cross_query = jnp.dot(grid_rows, query_weight, preferred_element_type=jnp.float32).astype(jnp.bfloat16)
    cross_query = cross_query.reshape(tile_count, cell_count, channels)
    sensor_keyval = jnp.dot(received.reshape(-1, F), sensor_weight, preferred_element_type=jnp.float32)
    sensor_keyval = sensor_keyval.astype(jnp.bfloat16).reshape(tile_count, SLOTS, 2 * channels)

    def cross_tile(inputs):
        return cross_forward(inputs[0], inputs[1], inputs[2], inputs[3], TH, TW, HEADS)
    cross_att, cross_total = lax.map(cross_tile, (cross_query, sensor_keyval, row_code, col_code))
    cross_flat = cross_att.reshape(-1, channels)
    after_cross = (grid_rows.astype(jnp.float32) + jnp.dot(cross_flat, cross_weight, preferred_element_type=jnp.float32)).astype(jnp.bfloat16)
    local_qkv = jnp.dot(after_cross, local_weight, preferred_element_type=jnp.float32).astype(jnp.bfloat16)
    local_qkv = local_qkv.reshape(tile_count, cell_count, 3 * channels)
    local_query = local_qkv[:, :, :channels]
    local_keyval = local_qkv[:, :, channels:]
    padded_kv = pad_rim(from_tiles(local_keyval))

    def local_tile(inputs):
        tile, queries = inputs
        allowed = make_window(tile // N_LON, N_LAT, TH, TW)
        return local_forward(queries, rim_tile(padded_kv, tile), allowed, HEADS)
    local_att, local_total = lax.map(local_tile, (tile_ids, local_query))
    local_flat = local_att.reshape(-1, channels)
    updated = (after_cross.astype(jnp.float32) + jnp.dot(local_flat, merge_weight, preferred_element_type=jnp.float32)).astype(jnp.bfloat16)
    grad_rows = to_tiles(cotangent).reshape(-1, channels)
    grad_merge_weight = jnp.dot(local_flat.T, grad_rows, preferred_element_type=jnp.float32)
    grad_local_att = jnp.dot(grad_rows, merge_weight.T, preferred_element_type=jnp.float32).astype(jnp.bfloat16)
    grad_local_att = grad_local_att.reshape(tile_count, cell_count, channels)

    def query_tile(inputs):
        tile, queries, head_total, grad_att = inputs
        allowed = make_window(tile // N_LON, N_LAT, TH, TW)
        return local_back_queries(queries, rim_tile(padded_kv, tile), allowed, head_total, grad_att, HEADS)
    grad_local_query, local_delta = lax.map(query_tile, (tile_ids, local_query, local_total, grad_local_att))
    padded_qga = pad_rim(from_tiles(jnp.concatenate([local_query, grad_local_att], axis=2)))
    padded_total = pad_rim(from_tiles(jnp.transpose(local_total, (0, 2, 1))))
    padded_delta = pad_rim(from_tiles(jnp.transpose(local_delta, (0, 2, 1))))

    def key_tile(inputs):
        tile, keyval = inputs
        allowed = make_window(tile // N_LON, N_LAT, TH, TW)
        query_grad = rim_tile(padded_qga, tile)
        return local_back_keys(keyval, query_grad[:, :channels], query_grad[:, channels:], rim_tile(padded_total, tile).T, rim_tile(padded_delta, tile).T, allowed, HEADS)
    grad_keys, grad_values = lax.map(key_tile, (tile_ids, local_keyval))
    grad_qkv = jnp.concatenate([grad_local_query, grad_keys, grad_values], axis=2).astype(jnp.bfloat16)
    grad_qkv = grad_qkv.reshape(-1, 3 * channels)
    grad_local_weight = jnp.dot(after_cross.T, grad_qkv, preferred_element_type=jnp.float32)
    grad_mixed = grad_rows.astype(jnp.float32) + jnp.dot(grad_qkv, local_weight.T, preferred_element_type=jnp.float32)
    grad_rounded = grad_mixed.astype(jnp.bfloat16)
    grad_cross_weight = jnp.dot(cross_flat.T, grad_rounded, preferred_element_type=jnp.float32)
    grad_cross_att = jnp.dot(grad_rounded, cross_weight.T, preferred_element_type=jnp.float32).astype(jnp.bfloat16)
    grad_cross_att = grad_cross_att.reshape(tile_count, cell_count, channels)

    def cross_back_tile(inputs):
        return cross_backward(inputs[0], inputs[1], inputs[2], inputs[3], inputs[4], inputs[5], TH, TW, HEADS)
    grad_cross_query, grad_sensor_kv = lax.map(cross_back_tile, (cross_query, sensor_keyval, row_code, col_code, cross_total, grad_cross_att))
    grad_query_flat = grad_cross_query.reshape(-1, channels)
    grad_query_weight = jnp.dot(grid_rows.T, grad_query_flat, preferred_element_type=jnp.float32)
    grad_grid = grad_mixed + jnp.dot(grad_query_flat, query_weight.T, preferred_element_type=jnp.float32)
    grad_kv_flat = grad_sensor_kv.reshape(-1, 2 * channels)
    grad_sensor_weight = jnp.dot(received.reshape(-1, F).T, grad_kv_flat, preferred_element_type=jnp.float32)
    grad_slots = jnp.dot(grad_kv_flat, sensor_weight.T, preferred_element_type=jnp.float32).astype(jnp.bfloat16)
    grad_observations = grad_slots[where_to]
    updated = from_tiles(updated.reshape(tile_count, cell_count, channels))
    grad_grid = from_tiles(grad_grid.reshape(tile_count, cell_count, channels))
    return (updated, grad_grid, grad_observations, grad_query_weight, grad_sensor_weight, grad_cross_weight, grad_local_weight, grad_merge_weight)
```

```python
import functools
import math

import jax
import jax.numpy as jnp
from jax import lax
from jax.experimental import pallas as pl
from jax.experimental.pallas import tpu as pltpu
from jax.sharding import Mesh
from jax.sharding import PartitionSpec as P

B16 = jnp.bfloat16
F32 = jnp.float32
HEADS = 16
WIDTH = 32
GROUP = 4
GROUPS = HEADS // GROUP
RADIUS = 6
TH = 8
TW = 16
CELLS = TH * TW
C = 512
F = 256
OBS = 256
TILES = 128
CAP = 6
PITCH = 8
SLOTS = TILES * CAP
WIRE = TILES * PITCH
NLAT = 64
EDGE = RADIUS * TW
SIDE = 128
REGION = CELLS + 2 * EDGE
KEYS = REGION + 2 * SIDE
SCALE = 1.0 / math.sqrt(WIDTH)
LOG2E = math.log2(math.e)
LANES = GROUP * CELLS
ROWS_A = 5120
ROWS_B = 2048
VMEM_LIMIT = 44 * 1024 * 1024

ALL = ("zlo", "x", "y", "zhi", "core")
CHIPS = ("zlo", "x", "y", "zhi")
LAT = ("zlo", "x")
LON = ("y", "zhi", "core")


def dot(a, b):
    return jnp.dot(a, b, preferred_element_type=F32)


def dot_nt(a, b):
    return lax.dot_general(a, b, (((1,), (1,)), ((), ())), preferred_element_type=F32)


def iota(shape, dim):
    return lax.broadcasted_iota(jnp.int32, shape, dim)


def one_hot(condition):
    return jnp.where(condition, 1.0, 0.0).astype(B16)


def sixth(index):
    return lax.shift_right_logical(index * 10923, 16)


def call(kernel, outs, args, scratch=(), scalars=0):
    vmem = pl.BlockSpec(memory_space=pltpu.VMEM)
    smem = pl.BlockSpec(memory_space=pltpu.SMEM)
    return pl.pallas_call(
        kernel,
        out_shape=tuple(jax.ShapeDtypeStruct(s, d) for s, d in outs),
        in_specs=[smem] * scalars + [vmem] * (len(args) - scalars),
        out_specs=tuple(vmem for _ in outs),
        scratch_shapes=list(scratch),
        compiler_params=pltpu.CompilerParams(vmem_limit_bytes=VMEM_LIMIT),
    )(*args)


def route_kernel(obs, tile_row, tile_col, cell_col, accept_col, out, slot):
    tcol, trow = tile_col[...], tile_row[...]
    hits = jnp.where(tcol == iota((OBS, TILES), 1), 1.0, 0.0)
    before = one_hot(iota((OBS, OBS), 0) > iota((OBS, OBS), 1))
    rank_col = jnp.sum(dot(before, hits.astype(B16)) * hits, axis=1, keepdims=True).astype(jnp.int32)
    hits_t = jnp.where(trow == iota((TILES, OBS), 0), 1.0, 0.0)
    after = one_hot(iota((OBS, OBS), 0) < iota((OBS, OBS), 1))
    rank_row = jnp.sum(dot(hits_t.astype(B16), after) * hits_t, axis=0, keepdims=True).astype(jnp.int32)
    slot[...] = tcol * PITCH + rank_col
    lane = iota((OBS, F), 1)
    cell = cell_col[...]
    row_code = ((lax.shift_right_logical(cell, 4) + 1) * accept_col[...]).astype(F32)
    col_code = (cell & (TW - 1)).astype(F32)
    codes = (
        jnp.where(lane == rank_col, row_code, 0.0) + jnp.where(lane == rank_col + 8, col_code, 0.0)
    ).astype(B16)
    wire = iota((WIRE, OBS), 0)
    placed = one_hot(wire == trow * PITCH + rank_row)
    coded = one_hot(wire == trow * PITCH + CAP)
    out[...] = (dot(placed, obs[...]) + dot(coded, codes)).astype(B16)


def masked_heads(block):
    lane = lax.shift_right_logical(iota(block.shape, 1), 5)
    zero = jnp.zeros_like(block)
    return jnp.concatenate([jnp.where(lane == h, block, zero) for h in range(GROUP)], axis=0)


def head_blocks(stacked):
    return jnp.concatenate(
        [stacked[h * WIDTH : (h + 1) * WIDTH, h * CELLS : (h + 1) * CELLS] for h in range(GROUP)],
        axis=0,
    ).T


def fold(x, op):
    return op(x.reshape(x.shape[0] // 8, 8, x.shape[1]), axis=0)


def slope_of(group, h):
    return jnp.exp2(jnp.full((1, CELLS), 3.0, F32) - 0.5 * (group * GROUP + h).astype(F32))


def cross_kernel(
    arrived, grid, query_w, sensor_w, cross_w, local_w,
    slots_out, keyval, query, prob, att, after, local_q, local_kv,
    gap, scores,
):
    slot = iota((SLOTS, WIRE), 0)
    source = sixth(slot)
    wire = iota((SLOTS, WIRE), 1)
    rows = arrived[...]
    picked = dot(one_hot(wire == slot + 2 * source), rows).astype(B16)
    codes = dot(one_hot(wire == source * PITCH + CAP), rows[:, :128])
    slots_out[...] = picked
    keyval[...] = dot(picked, sensor_w[...]).astype(B16)
    query[...] = dot(grid[...], query_w[...]).astype(B16)

    index = iota((SLOTS, 128), 0)
    rank = index - CAP * sixth(index)
    lane = iota((SLOTS, 128), 1)
    row_code = jnp.sum(jnp.where(lane == rank, codes, 0.0), axis=1, keepdims=True)
    col_code = jnp.sum(jnp.where(lane == rank + 8, codes, 0.0), axis=1, keepdims=True)
    cell_row = lax.shift_right_logical(lane, 4).astype(F32)
    cell_col = (lane & (TW - 1)).astype(F32)
    row_gap = (cell_row - (row_code - 1.0)) * (1.0 / TH)
    col_gap = (cell_col - col_code) * (1.0 / TW)
    gap[...] = jnp.where(row_code > 0.5, -(row_gap * row_gap + col_gap * col_gap), -1e30)

    step = 96

    def one_group(g, carry):
        lanes = pl.ds(pl.multiple_of(g * 128, 128), 128)
        values = keyval[:, pl.ds(pl.multiple_of(C + g * 128, 128), 128)]
        scores[...] = dot_nt(keyval[:, lanes], masked_heads(query[:, lanes]))
        for h in range(GROUP):
            cols = slice(h * CELLS, (h + 1) * CELLS)
            slope = slope_of(g, h) * LOG2E
            top = jnp.zeros((8, CELLS), F32)
            for r in range(0, SLOTS, step):
                s = scores[r : r + step, cols] * (SCALE * LOG2E) + slope * gap[r : r + step, :]
                scores[r : r + step, cols] = s
                top = jnp.maximum(top, fold(s, jnp.max))
            top = jnp.max(top, axis=0, keepdims=True)
            total = jnp.zeros((8, CELLS), F32)
            for r in range(0, SLOTS, step):
                e = jnp.exp2(scores[r : r + step, cols] - top)
                scores[r : r + step, cols] = e
                total = total + fold(e, jnp.sum)
            total = jnp.sum(total, axis=0, keepdims=True) + jnp.exp2(-top)
            inverse = 1.0 / total
            for r in range(0, SLOTS, step):
                prob[g, r : r + step, cols] = (scores[r : r + step, cols] * inverse).astype(B16)
        att[:, lanes] = head_blocks(dot(values.T, prob[g])).astype(B16)
        return carry

    lax.fori_loop(0, GROUPS, one_group, 0)
    mixed = (grid[...].astype(F32) + dot(att[...], cross_w[...])).astype(B16)
    after[...] = mixed
    qkv = dot(mixed, local_w[...]).astype(B16)
    local_q[...] = qkv[:, :C]
    local_kv[...] = qkv[:, C:]


def side_rows(shape, key_dim, first_col):
    key = iota(shape, key_dim)
    line = sixth(key)
    wanted = line * TW + first_col + key - CAP * line
    return (iota(shape, 1 - key_dim) == wanted) & (key < (TH + 2 * RADIUS) * RADIUS)


def edges_kernel(top, own, bottom, left, right):
    region = jnp.concatenate([top[...], own[...], bottom[...]], axis=0)
    shape = (SIDE, REGION)
    left[...] = dot(one_hot(side_rows(shape, 0, 0)), region).astype(B16)
    right[...] = dot(one_hot(side_rows(shape, 0, TW - RADIUS)), region).astype(B16)


def window(lat_index, shape, key_row, key_col, valid):
    lane = iota(shape, 1)
    row_gap = key_row - lax.shift_right_logical(lane, 4)
    col_gap = key_col - (lane & (TW - 1))
    global_row = lat_index * TH + key_row
    seen = (jnp.abs(row_gap) <= RADIUS) & (jnp.abs(col_gap) <= RADIUS)
    seen = seen & (global_row >= 0) & (global_row < NLAT) & valid
    return jnp.where(seen, 0.0, -1e30)


def local_kernel(
    lat_index, query, top, own, bottom, left, right, cotangent, merge_w, after,
    updated, att, grad_query, grad_region, grad_left, grad_right,
    keyval, bias, scores, grad_prob, prob, grad_score, grad_att,
):
    lat = lat_index[0]
    keyval[0:EDGE] = top[...]
    keyval[EDGE : EDGE + CELLS] = own[...]
    keyval[EDGE + CELLS : REGION] = bottom[...]
    keyval[REGION : REGION + SIDE] = left[...]
    keyval[REGION + SIDE : KEYS] = right[...]
    grad_att[...] = dot_nt(cotangent[...], merge_w[...]).astype(B16)
    key = iota((REGION, CELLS), 0)
    bias[0:REGION] = window(
        lat, (REGION, CELLS), lax.shift_right_logical(key, 4) - RADIUS, key & (TW - 1), key >= 0
    )
    key = iota((SIDE, CELLS), 0)
    line = sixth(key)
    offset = key - CAP * line
    valid = line < TH + 2 * RADIUS
    bias[REGION : REGION + SIDE] = window(
        lat, (SIDE, CELLS), line - RADIUS, offset - RADIUS, valid
    )
    bias[REGION + SIDE : KEYS] = window(lat, (SIDE, CELLS), line - RADIUS, offset + TW, valid)

    step = 96

    def one_group(g, carry):
        lanes = pl.ds(pl.multiple_of(g * 128, 128), 128)
        upper = pl.ds(pl.multiple_of(C + g * 128, 128), 128)
        keys, values = keyval[:, lanes], keyval[:, upper]
        heads_query = masked_heads(query[:, lanes])
        heads_grad = masked_heads(grad_att[:, lanes])
        scores[...] = dot_nt(keys, heads_query)
        grad_prob[...] = dot_nt(values, heads_grad)
        for h in range(GROUP):
            cols = slice(h * CELLS, (h + 1) * CELLS)
            top_score = jnp.full((8, CELLS), -1e30, F32)
            for r in range(0, KEYS, step):
                s = scores[r : r + step, cols] * (SCALE * LOG2E) + bias[r : r + step, :]
                scores[r : r + step, cols] = s
                top_score = jnp.maximum(top_score, fold(s, jnp.max))
            top_score = jnp.max(top_score, axis=0, keepdims=True)
            total = jnp.zeros((8, CELLS), F32)
            delta = jnp.zeros((8, CELLS), F32)
            for r in range(0, KEYS, step):
                e = jnp.exp2(scores[r : r + step, cols] - top_score)
                scores[r : r + step, cols] = e
                total = total + fold(e, jnp.sum)
                delta = delta + fold(e * grad_prob[r : r + step, cols], jnp.sum)
            inverse = 1.0 / jnp.sum(total, axis=0, keepdims=True)
            delta = jnp.sum(delta, axis=0, keepdims=True) * inverse
            for r in range(0, KEYS, step):
                p = scores[r : r + step, cols] * inverse
                prob[r : r + step, cols] = p.astype(B16)
                grad_score[r : r + step, cols] = (
                    p * (grad_prob[r : r + step, cols] - delta)
                ).astype(B16)
        att[:, lanes] = head_blocks(dot(values.T, prob[...])).astype(B16)
        grad_query[:, lanes] = head_blocks(dot(keys.T, grad_score[...])) * SCALE
        grad_key = dot(grad_score[...], heads_query) * SCALE
        grad_value = dot(prob[...], heads_grad)
        for part, where_to in ((grad_key, lanes), (grad_value, upper)):
            grad_region[:, where_to] = part[0:REGION]
            grad_left[:, where_to] = part[REGION : REGION + SIDE].astype(B16)
            grad_right[:, where_to] = part[REGION + SIDE : KEYS].astype(B16)
        return carry

    lax.fori_loop(0, GROUPS, one_group, 0)
    updated[...] = (after[...].astype(F32) + dot(att[...], merge_w[...])).astype(B16)


def gather_kernel(grad_region, from_left, from_right, top, own, bottom):
    shape = (REGION, SIDE)
    total = (
        grad_region[...]
        + dot(one_hot(side_rows(shape, 1, 0)), from_left[...])
        + dot(one_hot(side_rows(shape, 1, TW - RADIUS)), from_right[...])
    )
    top[...] = total[0:EDGE].astype(B16)
    own[...] = total[EDGE : EDGE + CELLS]
    bottom[...] = total[EDGE + CELLS : REGION].astype(B16)


def put_blocks(staged, first, product):
    height = product.shape[0]
    for i in range(product.shape[1] // 128):
        at = first + i * height
        half, row = at // staged.shape[1], at % staged.shape[1]
        staged[half, row : row + height] = product[:, i * 128 : (i + 1) * 128].astype(B16)


def split_halves(core, staged, mine, send):
    for half in range(2):

        @pl.when(core == half)
        def _(half=half):
            mine[...] = staged[half]

        @pl.when(core != half)
        def _(half=half):
            send[...] = staged[half]


def mixed_kernel(
    core_index, grad_query, grad_kv, from_above, from_below, cotangent, local_w, after, cross_att,
    cross_w, local_att,
    mine, send, grad_mixed, grad_cross_att,
    staged, keyval,
):
    keyval[...] = grad_kv[...]
    keyval[0:EDGE] = keyval[0:EDGE] + from_above[...].astype(F32)
    keyval[CELLS - EDGE :] = keyval[CELLS - EDGE :] + from_below[...].astype(F32)
    grad_qkv = jnp.concatenate([grad_query[...].astype(B16), keyval[...].astype(B16)], axis=1)
    put_blocks(staged, 0, dot(local_att[...].T, cotangent[...]))
    put_blocks(staged, 4 * C, dot(after[...].T, grad_qkv))
    mixed = cotangent[...].astype(F32) + dot_nt(grad_qkv, local_w[...])
    grad_mixed[...] = mixed
    rounded = mixed.astype(B16)
    put_blocks(staged, 16 * C, dot(cross_att[...].T, rounded))
    grad_cross_att[...] = dot_nt(rounded, cross_w[...]).astype(B16)
    split_halves(core_index[0], staged, mine, send)


def cross_back_kernel(
    core_index, query, keyval, prob, grad_att, grid, query_w, sensor_w, slots, grad_mixed,
    mine, send, grad_grid, grad_wire,
    staged, grad_prob, grad_score, grad_query, grad_keyval,
):
    step = 96

    def one_group(g, carry):
        lanes = pl.ds(pl.multiple_of(g * 128, 128), 128)
        upper = pl.ds(pl.multiple_of(C + g * 128, 128), 128)
        keys, values = keyval[:, lanes], keyval[:, upper]
        heads_query = masked_heads(query[:, lanes])
        heads_grad = masked_heads(grad_att[:, lanes])
        grad_prob[...] = dot_nt(values, heads_grad)
        for h in range(GROUP):
            cols = slice(h * CELLS, (h + 1) * CELLS)
            delta = jnp.zeros((8, CELLS), F32)
            for r in range(0, SLOTS, step):
                p = prob[g, r : r + step, cols].astype(F32)
                delta = delta + fold(p * grad_prob[r : r + step, cols], jnp.sum)
            delta = jnp.sum(delta, axis=0, keepdims=True)
            for r in range(0, SLOTS, step):
                p = prob[g, r : r + step, cols].astype(F32)
                grad_score[r : r + step, cols] = (
                    p * (grad_prob[r : r + step, cols] - delta)
                ).astype(B16)
        grad_query[:, lanes] = (head_blocks(dot(keys.T, grad_score[...])) * SCALE).astype(B16)
        grad_keyval[:, lanes] = (dot(grad_score[...], heads_query) * SCALE).astype(B16)
        grad_keyval[:, upper] = dot(prob[g], heads_grad).astype(B16)
        return carry

    lax.fori_loop(0, GROUPS, one_group, 0)
    grad_slots = dot_nt(grad_keyval[...], sensor_w[...]).astype(B16)
    wire, slot = iota((WIRE, SLOTS), 0), iota((WIRE, SLOTS), 1)
    source = sixth(slot)
    grad_wire[...] = dot(one_hot(wire == slot + 2 * source), grad_slots).astype(B16)
    put_blocks(staged, 0, dot(grid[...].T, grad_query[...]))
    put_blocks(staged, ROWS_B, dot(slots[...].T, grad_keyval[...]))
    grad_grid[...] = grad_mixed[...] + dot_nt(grad_query[...], query_w[...])
    split_halves(core_index[0], staged, mine, send)


def return_kernel(slot, returned, grad_obs):
    pick = one_hot(slot[...] == iota((OBS, WIRE), 1))
    grad_obs[...] = dot(pick, returned[...]).astype(B16)


def take_blocks(halves, first, out):
    height = out.shape[0]
    for i in range(out.shape[1] // 128):
        at = first + i * height
        half, row = at // halves[0].shape[0], at % halves[0].shape[0]
        out[:, i * 128 : (i + 1) * 128] = halves[half][row : row + height].astype(F32)


def unpack_kernel(starts, core_index, mine, other, *outs):
    for core in range(2):

        @pl.when(core_index[0] == core)
        def _(core=core):
            halves = (mine, other) if core == 0 else (other, mine)
            for start, out in zip(starts, outs, strict=True):
                take_blocks(halves, start, out)


CORE_PAIRS = ((0, 1), (1, 0))


def reduced_share(mine, send):
    partner = lax.ppermute(send, "core", CORE_PAIRS)
    pair = (mine.astype(F32) + partner.astype(F32)).astype(B16)
    chips = 64
    parts = lax.all_to_all(
        pair.reshape(chips, -1, 128), CHIPS, split_axis=0, concat_axis=0, tiled=True
    )
    return jnp.sum(parts.astype(F32), axis=0).astype(B16)


def gathered_halves(share):
    chips = 64
    spread = jnp.broadcast_to(share[None], (chips,) + share.shape)
    mine = lax.all_to_all(spread, CHIPS, split_axis=0, concat_axis=0, tiled=True).reshape(-1, 128)
    return mine, lax.ppermute(mine, "core", CORE_PAIRS)


def on_device(
    grid_state, observations, target_tile, target_cell, accepted,
    query_weight, sensor_weight, cross_weight, local_weight, merge_weight, cotangent,
):
    lat = lax.axis_index(LAT).astype(jnp.int32).reshape(1)
    core = lax.axis_index("core").astype(jnp.int32).reshape(1)
    lat_count, lon_count = NLAT // TH, TILES * TH // NLAT
    down = [(i, i + 1) for i in range(lat_count - 1)]
    up = [(i + 1, i) for i in range(lat_count - 1)]
    east = [(i, (i + 1) % lon_count) for i in range(lon_count)]
    west = [((i + 1) % lon_count, i) for i in range(lon_count)]
    grid = grid_state.reshape(CELLS, C)
    grad_rows = cotangent.reshape(CELLS, C)

    outgoing, slot = call(
        route_kernel,
        [((WIRE, F), B16), ((OBS, 1), jnp.int32)],
        (
            observations, target_tile.reshape(1, OBS), target_tile,
            target_cell.reshape(OBS, 1), accepted.reshape(OBS, 1),
        ),
    )
    arrived = lax.all_to_all(
        outgoing.reshape(TILES, PITCH, F), ALL, split_axis=0, concat_axis=0, tiled=True
    ).reshape(WIRE, F)

    slots, keyval, query, prob, cross_att, after, local_q, local_kv = call(
        cross_kernel,
        [
            ((SLOTS, F), B16), ((SLOTS, 2 * C), B16), ((CELLS, C), B16),
            ((GROUPS, SLOTS, LANES), B16), ((CELLS, C), B16), ((CELLS, C), B16),
            ((CELLS, C), B16), ((CELLS, 2 * C), B16),
        ],
        (arrived, grid, query_weight, sensor_weight, cross_weight, local_weight),
        scratch=[pltpu.VMEM((SLOTS, CELLS), F32), pltpu.VMEM((SLOTS, LANES), F32)],
    )

    top = lax.ppermute(local_kv[CELLS - EDGE :], LAT, down)
    bottom = lax.ppermute(local_kv[:EDGE], LAT, up)
    send_left, send_right = call(
        edges_kernel,
        [((SIDE, 2 * C), B16), ((SIDE, 2 * C), B16)],
        (top, local_kv, bottom),
    )
    left = lax.ppermute(send_right, LON, east)
    right = lax.ppermute(send_left, LON, west)

    updated, local_att, grad_query, grad_region, grad_left, grad_right = call(
        local_kernel,
        [
            ((CELLS, C), B16), ((CELLS, C), B16), ((CELLS, C), F32),
            ((REGION, 2 * C), F32), ((SIDE, 2 * C), B16), ((SIDE, 2 * C), B16),
        ],
        (
            lat, local_q, top, local_kv, bottom, left, right, grad_rows, merge_weight, after,
        ),
        scratch=[
            pltpu.VMEM((KEYS, 2 * C), B16), pltpu.VMEM((KEYS, CELLS), F32),
            pltpu.VMEM((KEYS, LANES), F32), pltpu.VMEM((KEYS, LANES), F32),
            pltpu.VMEM((KEYS, LANES), B16), pltpu.VMEM((KEYS, LANES), B16),
            pltpu.VMEM((CELLS, C), B16),
        ],
        scalars=1,
    )
    back_right = lax.ppermute(grad_left, LON, west)
    back_left = lax.ppermute(grad_right, LON, east)
    grad_top, grad_own, grad_bottom = call(
        gather_kernel,
        [((EDGE, 2 * C), B16), ((CELLS, 2 * C), F32), ((EDGE, 2 * C), B16)],
        (grad_region, back_left, back_right),
    )
    from_below = lax.ppermute(grad_top, LAT, up)
    from_above = lax.ppermute(grad_bottom, LAT, down)

    mine_a, send_a, grad_mixed, grad_cross_att = call(
        mixed_kernel,
        [
            ((ROWS_A, 128), B16), ((ROWS_A, 128), B16), ((CELLS, C), F32), ((CELLS, C), B16),
        ],
        (
            core, grad_query, grad_own, from_above, from_below, grad_rows, local_weight, after,
            cross_att, cross_weight, local_att,
        ),
        scratch=[pltpu.VMEM((2, ROWS_A, 128), B16), pltpu.VMEM((CELLS, 2 * C), F32)],
        scalars=1,
    )
    mine_b, send_b, grad_grid, grad_wire = call(
        cross_back_kernel,
        [
            ((ROWS_B, 128), B16), ((ROWS_B, 128), B16), ((CELLS, C), F32), ((WIRE, F), B16),
        ],
        (
            core, query, keyval, prob, grad_cross_att, grid, query_weight, sensor_weight, slots,
            grad_mixed,
        ),
        scratch=[
            pltpu.VMEM((2, ROWS_B, 128), B16), pltpu.VMEM((SLOTS, LANES), F32),
            pltpu.VMEM((SLOTS, LANES), B16), pltpu.VMEM((CELLS, C), B16),
            pltpu.VMEM((SLOTS, 2 * C), B16),
        ],
        scalars=1,
    )
    share_a = reduced_share(mine_a, send_a)
    returned = lax.all_to_all(
        grad_wire.reshape(TILES, PITCH, F), ALL, split_axis=0, concat_axis=0, tiled=True
    ).reshape(WIRE, F)
    share_b = reduced_share(mine_b, send_b)
    (grad_obs,) = call(return_kernel, [((OBS, F), B16)], (slot, returned))
    grad_merge, grad_local, grad_cross = call(
        functools.partial(unpack_kernel, (0, 4 * C, 16 * C)),
        [((C, C), F32), ((C, 3 * C), F32), ((C, C), F32)],
        (core, *gathered_halves(share_a)),
        scalars=1,
    )
    grad_query_w, grad_sensor = call(
        functools.partial(unpack_kernel, (0, ROWS_B)),
        [((C, C), F32), ((F, 2 * C), F32)],
        (core, *gathered_halves(share_b)),
        scalars=1,
    )
    return (
        updated.reshape(TH, TW, C), grad_grid.reshape(TH, TW, C), grad_obs,
        grad_query_w, grad_sensor, grad_cross, grad_local, grad_merge,
    )


def solution(mesh):
    fine = Mesh(mesh.devices.reshape(2, 4, 4, 2, 2), ALL)
    in_specs = (
        P(LAT, LON, None), P(ALL, None), P(ALL, None), P(ALL), P(ALL),
        P(), P(), P(), P(), P(), P(LAT, LON, None),
    )
    out_specs = (P(LAT, LON, None), P(LAT, LON, None), P(ALL, None), P(), P(), P(), P(), P())
    return jax.shard_map(
        on_device, mesh=fine, in_specs=in_specs, out_specs=out_specs, check_vma=False
    )
```

```python
import math

import jax
import jax.numpy as jnp
from jax import lax
from jax.experimental import pallas as pl
from jax.experimental.pallas import tpu as pltpu
from jax.sharding import Mesh
from jax.sharding import PartitionSpec as P

B16 = jnp.bfloat16
F32 = jnp.float32
HEADS = 16
WIDTH = 32
GROUP = 4
GROUPS = HEADS // GROUP
RADIUS = 6
TH = 8
TW = 16
CELLS = TH * TW
C = 512
F = 256
OBS = 256
TILES = 128
CAP = 6
PITCH = 8
SLOTS = TILES * CAP
WIRE = TILES * PITCH
NLAT = 64
EDGE = RADIUS * TW
SIDE = 128
REGION = CELLS + 2 * EDGE
KEYS = REGION + 2 * SIDE
SCALE = 1.0 / math.sqrt(WIDTH)
LOG2E = math.log2(math.e)
LANES = GROUP * CELLS
SIDE_COUNT = 8
RING = 4
ROWS_CELLS = 5120
ROWS_LATE = 2048

ALL = ("zlo", "x", "y", "zhi", "core")
LAT = ("zlo", "x")
DEPTH = ("zlo", "zhi")
LON = ("y", "zhi", "core")
SECTOR = ("y", "zhi")


def dot(a, b):
    return jnp.dot(a, b, preferred_element_type=F32)


def dot_nt(a, b):
    return lax.dot_general(a, b, (((1,), (1,)), ((), ())), preferred_element_type=F32)


def iota(shape, dim):
    return lax.broadcasted_iota(jnp.int32, shape, dim)


def one_hot(condition):
    return jnp.where(condition, 1.0, 0.0).astype(B16)


def sixth(index):
    return lax.shift_right_logical(index * 10923, 16)


class Arriving:
    def __init__(self, source, buffer, semaphore):
        self.copy = pltpu.make_async_copy(source, buffer, semaphore)
        self.copy.start()
        self.buffer = buffer

    def __call__(self):
        self.copy.wait()
        return self.buffer


def call(
    kernel, outs, args, scratch=(), scalars=0, micros=1, after=(), loads=(), saves=(), raw=(),
    raw_outs=(), megabytes=16,
):
    vmem = pl.BlockSpec(memory_space=pltpu.VMEM)
    smem = pl.BlockSpec(memory_space=pltpu.SMEM)
    hbm = pl.BlockSpec(memory_space=pltpu.HBM)
    count, late, given, own = len(args), len(after), len(outs), len(scratch)

    def body(*refs):
        ins = list(refs[:count])
        results = list(refs[count + late : count + late + given])
        rest = refs[count + late + given :]
        held, rest = rest[:own], rest[own:]
        buffers, rest = rest[: len(loads) + len(saves)], rest[len(loads) + len(saves) :]
        semaphores = rest[0] if rest else None
        for k, i in enumerate(loads):
            ins[i] = Arriving(ins[i], buffers[k], semaphores.at[k])
        targets = list(results)
        for k, i in enumerate(saves):
            results[i] = buffers[len(loads) + k]
        kernel(*ins, *results, *held)
        leaving = [
            pltpu.make_async_copy(results[i], targets[i], semaphores.at[len(loads) + k])
            for k, i in enumerate(saves)
        ]
        for copy in leaving:
            copy.start()
        for copy in leaving:
            copy.wait()

    def spec_in(i):
        if i < scalars:
            return smem
        return hbm if i in loads or i in raw else vmem

    extra = [pltpu.VMEM(args[i].shape, args[i].dtype) for i in loads]
    extra += [pltpu.VMEM(*outs[i]) for i in saves]
    if extra:
        extra.append(pltpu.SemaphoreType.DMA((len(extra),)))
    return pl.pallas_call(
        body,
        out_shape=tuple(jax.ShapeDtypeStruct(s, d) for s, d in outs),
        in_specs=[spec_in(i) for i in range(count)]
        + [pl.BlockSpec(memory_space=pl.ANY)] * late,
        out_specs=tuple(hbm if i in saves or i in raw_outs else vmem for i in range(given)),
        scratch_shapes=list(scratch) + extra,
        compiler_params=pltpu.CompilerParams(vmem_limit_bytes=megabytes * 1024 * 1024),
        cost_estimate=pl.CostEstimate(
            flops=int(micros * 1e9), bytes_accessed=0, transcendentals=0
        ),
    )(*args, *after)


def as_column(row):
    return jnp.broadcast_to(row.astype(F32), (128, OBS)).T[:, :1].astype(jnp.int32)


def route_kernel(obs, tile_row, cell_row, accept_row, out, slot):
    trow = tile_row[...]
    tcol = as_column(trow)
    hits = jnp.where(tcol == iota((OBS, TILES), 1), 1.0, 0.0)
    before = one_hot(iota((OBS, OBS), 0) > iota((OBS, OBS), 1))
    rank_col = jnp.sum(dot(before, hits.astype(B16)) * hits, axis=1, keepdims=True).astype(jnp.int32)
    hits_t = jnp.where(trow == iota((TILES, OBS), 0), 1.0, 0.0)
    after = one_hot(iota((OBS, OBS), 0) < iota((OBS, OBS), 1))
    rank_row = jnp.sum(dot(hits_t.astype(B16), after) * hits_t, axis=0, keepdims=True).astype(jnp.int32)
    slot[...] = tcol * PITCH + rank_col
    lane = iota((OBS, F), 1)
    cell = as_column(cell_row[...])
    row_code = ((lax.shift_right_logical(cell, 4) + 1) * as_column(accept_row[...])).astype(F32)
    col_code = (cell & (TW - 1)).astype(F32)
    codes = (
        jnp.where(lane == rank_col, row_code, 0.0) + jnp.where(lane == rank_col + 8, col_code, 0.0)
    ).astype(B16)
    wire = iota((WIRE, OBS), 0)
    placed = one_hot(wire == trow * PITCH + rank_row)
    coded = one_hot(wire == trow * PITCH + CAP)
    out[...] = (dot(placed, obs[...]) + dot(coded, codes)).astype(B16)


def masked_heads(block):
    lane = lax.shift_right_logical(iota(block.shape, 1), 5)
    zero = jnp.zeros_like(block)
    return jnp.concatenate([jnp.where(lane == h, block, zero) for h in range(GROUP)], axis=0)


def head_blocks(stacked):
    return jnp.concatenate(
        [stacked[h * WIDTH : (h + 1) * WIDTH, h * CELLS : (h + 1) * CELLS] for h in range(GROUP)],
        axis=0,
    ).T


def fold(x, op):
    return op(x.reshape(x.shape[0] // 8, 8, x.shape[1]), axis=0)


def slope_of(group, h):
    return jnp.exp2(jnp.full((1, CELLS), 3.0, F32) - 0.5 * (group * GROUP + h).astype(F32))


def cross_kernel(
    arrived, grid, query_w, sensor_w, cross_w, local_w,
    slots_out, keyval, query, prob, att, after, local_q, local_kv,
    gap, scores,
):
    slot = iota((SLOTS, WIRE), 0)
    source = sixth(slot)
    wire = iota((SLOTS, WIRE), 1)
    rows = arrived[...]
    picked = dot(one_hot(wire == slot + 2 * source), rows).astype(B16)
    codes = dot(one_hot(wire == source * PITCH + CAP), rows[:, :128])
    slots_out[...] = picked
    keyval[...] = dot(picked, sensor_w[...]).astype(B16)
    query[...] = dot(grid[...], query_w[...]).astype(B16)

    index = iota((SLOTS, 128), 0)
    rank = index - CAP * sixth(index)
    lane = iota((SLOTS, 128), 1)
    row_code = jnp.sum(jnp.where(lane == rank, codes, 0.0), axis=1, keepdims=True)
    col_code = jnp.sum(jnp.where(lane == rank + 8, codes, 0.0), axis=1, keepdims=True)
    cell_row = lax.shift_right_logical(lane, 4).astype(F32)
    cell_col = (lane & (TW - 1)).astype(F32)
    row_gap = (cell_row - (row_code - 1.0)) * (1.0 / TH)
    col_gap = (cell_col - col_code) * (1.0 / TW)
    gap[...] = jnp.where(row_code > 0.5, -(row_gap * row_gap + col_gap * col_gap), -1e30)

    step = 96

    def one_group(g, carry):
        lanes = pl.ds(pl.multiple_of(g * 128, 128), 128)
        values = keyval[:, pl.ds(pl.multiple_of(C + g * 128, 128), 128)]
        scores[...] = dot_nt(keyval[:, lanes], masked_heads(query[:, lanes]))
        for h in range(GROUP):
            cols = slice(h * CELLS, (h + 1) * CELLS)
            slope = slope_of(g, h) * LOG2E
            top = jnp.zeros((8, CELLS), F32)
            for r in range(0, SLOTS, step):
                s = scores[r : r + step, cols] * (SCALE * LOG2E) + slope * gap[r : r + step, :]
                scores[r : r + step, cols] = s
                top = jnp.maximum(top, fold(s, jnp.max))
            top = jnp.max(top, axis=0, keepdims=True)
            total = jnp.zeros((8, CELLS), F32)
            for r in range(0, SLOTS, step):
                e = jnp.exp2(scores[r : r + step, cols] - top)
                scores[r : r + step, cols] = e
                total = total + fold(e, jnp.sum)
            total = jnp.sum(total, axis=0, keepdims=True) + jnp.exp2(-top)
            inverse = 1.0 / total
            for r in range(0, SLOTS, step):
                prob[g, r : r + step, cols] = (scores[r : r + step, cols] * inverse).astype(B16)
        att[:, lanes] = head_blocks(dot(values.T, prob[g])).astype(B16)
        return carry

    lax.fori_loop(0, GROUPS, one_group, 0)
    mixed = (grid[...].astype(F32) + dot(att[...], cross_w[...])).astype(B16)
    after[...] = mixed
    qkv = dot(mixed, local_w[...]).astype(B16)
    local_q[...] = qkv[:, :C]
    local_kv[...] = qkv[:, C:]


def side_rows(shape, key_dim, first_col):
    key = iota(shape, key_dim)
    line = sixth(key)
    wanted = line * TW + first_col + key - CAP * line
    return (iota(shape, 1 - key_dim) == wanted) & (key < (TH + 2 * RADIUS) * RADIUS)


def edges_kernel(top, own, bottom, left, right):
    region = jnp.concatenate([top[...], own[...], bottom[...]], axis=0)
    shape = (SIDE, REGION)
    left[...] = dot(one_hot(side_rows(shape, 0, 0)), region).astype(B16)
    right[...] = dot(one_hot(side_rows(shape, 0, TW - RADIUS)), region).astype(B16)


def window(lat_index, shape, key_row, key_col, valid):
    lane = iota(shape, 1)
    row_gap = key_row - lax.shift_right_logical(lane, 4)
    col_gap = key_col - (lane & (TW - 1))
    global_row = lat_index * TH + key_row
    seen = (jnp.abs(row_gap) <= RADIUS) & (jnp.abs(col_gap) <= RADIUS)
    seen = seen & (global_row >= 0) & (global_row < NLAT) & valid
    return jnp.where(seen, 0.0, -1e30)


def local_kernel(
    lat_index, query, top, own, bottom, left, right, cotangent, merge_w, after,
    updated, att, grad_query, grad_region, grad_left, grad_right,
    keyval, bias, scores, grad_prob, prob, grad_score, grad_att,
):
    lat = lat_index[0]
    keyval[0:EDGE] = top[...]
    keyval[EDGE : EDGE + CELLS] = own[...]
    keyval[EDGE + CELLS : REGION] = bottom[...]
    keyval[REGION : REGION + SIDE] = left[...]
    keyval[REGION + SIDE : KEYS] = right[...]
    grad_att[...] = dot_nt(cotangent[...], merge_w[...]).astype(B16)
    key = iota((REGION, CELLS), 0)
    bias[0:REGION] = window(
        lat, (REGION, CELLS), lax.shift_right_logical(key, 4) - RADIUS, key & (TW - 1), key >= 0
    )
    key = iota((SIDE, CELLS), 0)
    line = sixth(key)
    offset = key - CAP * line
    valid = line < TH + 2 * RADIUS
    bias[REGION : REGION + SIDE] = window(
        lat, (SIDE, CELLS), line - RADIUS, offset - RADIUS, valid
    )
    bias[REGION + SIDE : KEYS] = window(lat, (SIDE, CELLS), line - RADIUS, offset + TW, valid)

    step = 96

    def one_group(g, carry):
        lanes = pl.ds(pl.multiple_of(g * 128, 128), 128)
        upper = pl.ds(pl.multiple_of(C + g * 128, 128), 128)
        keys, values = keyval[:, lanes], keyval[:, upper]
        heads_query = masked_heads(query[:, lanes])
        heads_grad = masked_heads(grad_att[:, lanes])
        scores[...] = dot_nt(keys, heads_query)
        grad_prob[...] = dot_nt(values, heads_grad)
        for h in range(GROUP):
            cols = slice(h * CELLS, (h + 1) * CELLS)
            top_score = jnp.full((8, CELLS), -1e30, F32)
            for r in range(0, KEYS, step):
                s = scores[r : r + step, cols] * (SCALE * LOG2E) + bias[r : r + step, :]
                scores[r : r + step, cols] = s
                top_score = jnp.maximum(top_score, fold(s, jnp.max))
            top_score = jnp.max(top_score, axis=0, keepdims=True)
            total = jnp.zeros((8, CELLS), F32)
            delta = jnp.zeros((8, CELLS), F32)
            for r in range(0, KEYS, step):
                e = jnp.exp2(scores[r : r + step, cols] - top_score)
                scores[r : r + step, cols] = e
                total = total + fold(e, jnp.sum)
                delta = delta + fold(e * grad_prob[r : r + step, cols], jnp.sum)
            inverse = 1.0 / jnp.sum(total, axis=0, keepdims=True)
            delta = jnp.sum(delta, axis=0, keepdims=True) * inverse
            for r in range(0, KEYS, step):
                p = scores[r : r + step, cols] * inverse
                prob[r : r + step, cols] = p.astype(B16)
                grad_score[r : r + step, cols] = (
                    p * (grad_prob[r : r + step, cols] - delta)
                ).astype(B16)
        att[:, lanes] = head_blocks(dot(values.T, prob[...])).astype(B16)
        grad_query[:, lanes] = (head_blocks(dot(keys.T, grad_score[...])) * SCALE).astype(B16)
        grad_key = dot(grad_score[...], heads_query) * SCALE
        grad_value = dot(prob[...], heads_grad)
        for part, where_to in ((grad_key, lanes), (grad_value, upper)):
            grad_region[:, where_to] = part[0:REGION]
            grad_left[:, where_to] = part[REGION : REGION + SIDE].astype(B16)
            grad_right[:, where_to] = part[REGION + SIDE : KEYS].astype(B16)
        return carry

    lax.fori_loop(0, GROUPS, one_group, 0)
    updated[...] = (after[...].astype(F32) + dot(att[...], merge_w[...])).astype(B16)


def gather_kernel(grad_region, from_left, from_right, top, own, bottom):
    shape = (REGION, SIDE)
    total = (
        grad_region[...]
        + dot(one_hot(side_rows(shape, 1, 0)), from_left[...])
        + dot(one_hot(side_rows(shape, 1, TW - RADIUS)), from_right[...])
    )
    top[...] = total[0:EDGE].astype(B16)
    own[...] = total[EDGE : EDGE + CELLS]
    bottom[...] = total[EDGE + CELLS : REGION].astype(B16)


def put_blocks(staged, first, product):
    height = product.shape[0]
    for i in range(product.shape[1] // 128):
        at = first + i * height
        half, row = at // staged.shape[1], at % staged.shape[1]
        staged[half, row : row + height] = product[:, i * 128 : (i + 1) * 128].astype(B16)


def split_halves(core, staged, mine, send):
    for half in range(2):

        @pl.when(core == half)
        def _(half=half):
            mine[...] = staged[half]

        @pl.when(core != half)
        def _(half=half):
            send[...] = staged[half]


def mixed_kernel(
    core_index, grad_query, grad_kv, from_above, from_below, local_att, cotangent_in, local_in,
    after_in, cross_att_in, cross_in,
    mine, send, grad_mixed, grad_cross_att,
    staged, keyval,
):
    keyval[...] = grad_kv[...]
    keyval[0:EDGE] = keyval[0:EDGE] + from_above[...].astype(F32)
    keyval[CELLS - EDGE :] = keyval[CELLS - EDGE :] + from_below[...].astype(F32)
    grad_qkv = jnp.concatenate([grad_query[...], keyval[...].astype(B16)], axis=1)
    cotangent = cotangent_in()
    put_blocks(staged, 0, dot(local_att[...].T, cotangent[...]))
    put_blocks(staged, 4 * C, dot(after_in()[...].T, grad_qkv))
    mixed = cotangent[...].astype(F32) + dot_nt(grad_qkv, local_in()[...])
    grad_mixed[...] = mixed
    rounded = mixed.astype(B16)
    put_blocks(staged, 16 * C, dot(cross_att_in()[...].T, rounded))
    grad_cross_att[...] = dot_nt(rounded, cross_in()[...]).astype(B16)
    split_halves(core_index[0], staged, mine, send)


def cross_back_kernel(
    core_index, query_in, keyval_in, prob_in, grad_att, grid, query_w, sensor_w, slots, grad_mixed,
    mine, send, grad_grid, grad_wire,
    staged, grad_prob, grad_score, grad_query, grad_keyval, prob, prob_came,
):
    for g in range(GROUPS):
        pltpu.make_async_copy(prob_in.at[g], prob.at[g], prob_came.at[g]).start()
    query, keyval = query_in(), keyval_in()
    step = 96

    def one_group(g, carry):
        lanes = pl.ds(pl.multiple_of(g * 128, 128), 128)
        upper = pl.ds(pl.multiple_of(C + g * 128, 128), 128)
        keys, values = keyval[:, lanes], keyval[:, upper]
        heads_query = masked_heads(query[:, lanes])
        heads_grad = masked_heads(grad_att[:, lanes])
        grad_prob[...] = dot_nt(values, heads_grad)
        pltpu.make_async_copy(prob_in.at[g], prob.at[g], prob_came.at[g]).wait()
        for h in range(GROUP):
            cols = slice(h * CELLS, (h + 1) * CELLS)
            delta = jnp.zeros((8, CELLS), F32)
            for r in range(0, SLOTS, step):
                p = prob[g, r : r + step, cols].astype(F32)
                delta = delta + fold(p * grad_prob[r : r + step, cols], jnp.sum)
            delta = jnp.sum(delta, axis=0, keepdims=True)
            for r in range(0, SLOTS, step):
                p = prob[g, r : r + step, cols].astype(F32)
                grad_score[r : r + step, cols] = (
                    p * (grad_prob[r : r + step, cols] - delta)
                ).astype(B16)
        grad_query[:, lanes] = (head_blocks(dot(keys.T, grad_score[...])) * SCALE).astype(B16)
        grad_keyval[:, lanes] = (dot(grad_score[...], heads_query) * SCALE).astype(B16)
        grad_keyval[:, upper] = dot(prob[g], heads_grad).astype(B16)
        return carry

    lax.fori_loop(0, GROUPS, one_group, 0)
    grad_slots = dot_nt(grad_keyval[...], sensor_w()[...]).astype(B16)
    wire, slot = iota((WIRE, SLOTS), 0), iota((WIRE, SLOTS), 1)
    source = sixth(slot)
    grad_wire[...] = dot(one_hot(wire == slot + 2 * source), grad_slots).astype(B16)
    put_blocks(staged, 0, dot(grid()[...].T, grad_query[...]))
    put_blocks(staged, ROWS_LATE, dot(slots()[...].T, grad_keyval[...]))
    grad_grid[...] = grad_mixed()[...] + dot_nt(grad_query[...], query_w()[...])
    split_halves(core_index[0], staged, mine, send)


def return_kernel(slot, returned, grad_obs):
    pick = one_hot(slot[...] == iota((OBS, WIRE), 1))
    grad_obs[...] = dot(pick, returned[...]).astype(B16)


def take_blocks(halves, first, out):
    height = out.shape[0]
    for i in range(out.shape[1] // 128):
        at = first + i * height
        half, row = at // halves[0].shape[0], at % halves[0].shape[0]
        out[:, i * 128 : (i + 1) * 128] = halves[half][row : row + height].astype(F32)


def either_core(core, pairs, write):
    for index in range(2):

        @pl.when(core == index)
        def _(index=index):
            write(*[(mine, other) if index == 0 else (other, mine) for mine, other in pairs])


def unpack_cells_kernel(core_index, mine, other, merge, local, cross):
    def write(halves):
        take_blocks(halves, 0, merge)
        take_blocks(halves, 4 * C, local)
        take_blocks(halves, 16 * C, cross)

    either_core(core_index[0], ((mine, other),), write)


def unpack_late_kernel(core_index, mine, other, query, sensor):
    def write(halves):
        take_blocks(halves, 0, query)
        take_blocks(halves, ROWS_LATE, sensor)

    either_core(core_index[0], ((mine, other),), write)


def summed_parts(parts):
    total = parts[0].astype(F32)
    for i in range(1, SIDE_COUNT):
        total = total + parts[i].astype(F32)
    return total.astype(B16)


def spread_kernel(at, *refs):
    parts, spread = refs[:RING], refs[RING]
    rows = parts[0].shape[0]
    for shift, part in enumerate(parts):
        block = part[...]
        for i in range(SIDE_COUNT):
            spread[i, chunk(ring_place(at[0], -shift), rows)] = block


def hold_kernel(block, same):
    same[...] = block[...]


def ring_place(at, shift):
    return (at + shift) & (RING - 1)


def chunk(index, rows):
    return pl.ds(pl.multiple_of(index * rows, rows), rows)


def first_kernel(at, mine, partner, *pieces):
    rows = pieces[0].shape[0]
    for shift, piece in enumerate(pieces):
        block = chunk(ring_place(at[0], shift), rows)
        piece[...] = (mine[block].astype(F32) + partner[block].astype(F32)).astype(B16)


def band_kernel(at, bands, *refs):
    pieces, band = refs[:RING], refs[RING]
    band[...] = summed_parts(bands)
    rows = pieces[0].shape[0]
    for shift, piece in enumerate(pieces):
        piece[...] = band[chunk(ring_place(at[0], shift), rows)]


def summed(parts):
    total = parts[0][...].astype(F32)
    for part in parts[1:]:
        total = total + part[...].astype(F32)
    return total


def next_kernel(at, *refs):
    parts, pieces, total = refs[:RING], refs[RING : 2 * RING], refs[-1]
    total[...] = summed(parts)
    rows = pieces[0].shape[0]
    for shift, piece in enumerate(pieces):
        piece[...] = total[chunk(ring_place(at[0], shift), rows)].astype(B16)


def sum_kernel(*refs):
    refs[-1][...] = summed(refs[:-1]).astype(B16)


def ordered_sum_kernel(at, *refs):
    parts, out, held = refs[:RING], refs[RING], refs[RING + 1]
    for shift, part in enumerate(parts):
        held[ring_place(at[0], -shift)] = part[...].astype(F32)
    out[...] = (((held[0] + held[1]) + held[2]) + held[3]).astype(B16)


def joined_kernel(at, *refs):
    parts, out = refs[:RING], refs[RING]
    rows = parts[0].shape[0]
    for shift, part in enumerate(parts):
        out[chunk(ring_place(at[0], -shift), rows)] = part[...]


def ring_sends(axis, pieces):
    return [pieces[0]] + [
        lax.ppermute(piece, axis, [(i, (i + shift) % RING) for i in range(RING)])
        for shift, piece in enumerate(pieces)
        if shift
    ]


def spot(axis):
    return lax.axis_index(axis).astype(jnp.int32).reshape(1)


def some(rows, count):
    return [((rows, 128), B16)] * count


CORE_PAIRS = ((0, 1), (1, 0))


def swapped_parts(blocks, axes):
    return lax.all_to_all(blocks, axes, split_axis=0, concat_axis=0, tiled=True)


def on_device(
    grid_state, observations, target_tile, target_cell, accepted,
    query_weight, sensor_weight, cross_weight, local_weight, merge_weight, cotangent,
):
    lat = lax.axis_index(LAT).astype(jnp.int32).reshape(1)
    core = lax.axis_index("core").astype(jnp.int32).reshape(1)
    lat_count, lon_count = NLAT // TH, TILES * TH // NLAT
    down = [(i, i + 1) for i in range(lat_count - 1)]
    up = [(i + 1, i) for i in range(lat_count - 1)]
    east = [(i, (i + 1) % lon_count) for i in range(lon_count)]
    west = [((i + 1) % lon_count, i) for i in range(lon_count)]
    grid = grid_state.reshape(CELLS, C)
    grad_rows = cotangent.reshape(CELLS, C)

    outgoing, slot = call(
        route_kernel,
        [((WIRE, F), B16), ((OBS, 1), jnp.int32)],
        (
            observations, target_tile.reshape(1, OBS), target_cell.reshape(1, OBS),
            accepted.reshape(1, OBS),
        ),
    )
    arrived = lax.all_to_all(
        outgoing.reshape(TILES, PITCH, F), ALL, split_axis=0, concat_axis=0, tiled=True
    ).reshape(WIRE, F)

    slots, keyval, query, prob, cross_att, after, local_q, local_kv = call(
        cross_kernel,
        [
            ((SLOTS, F), B16), ((SLOTS, 2 * C), B16), ((CELLS, C), B16),
            ((GROUPS, SLOTS, LANES), B16), ((CELLS, C), B16), ((CELLS, C), B16),
            ((CELLS, C), B16), ((CELLS, 2 * C), B16),
        ],
        (arrived, grid, query_weight, sensor_weight, cross_weight, local_weight),
        scratch=[pltpu.VMEM((SLOTS, CELLS), F32), pltpu.VMEM((SLOTS, LANES), F32)],
        micros=7,
    )

    top = lax.ppermute(local_kv[CELLS - EDGE :], LAT, down)
    bottom = lax.ppermute(local_kv[:EDGE], LAT, up)
    send_left, send_right = call(
        edges_kernel,
        [((SIDE, 2 * C), B16), ((SIDE, 2 * C), B16)],
        (top, local_kv, bottom),
    )
    left = lax.ppermute(send_right, LON, east)
    right = lax.ppermute(send_left, LON, west)

    updated, local_att, grad_query, grad_region, grad_left, grad_right = call(
        local_kernel,
        [
            ((CELLS, C), B16), ((CELLS, C), B16), ((CELLS, C), B16),
            ((REGION, 2 * C), F32), ((SIDE, 2 * C), B16), ((SIDE, 2 * C), B16),
        ],
        (
            lat, local_q, top, local_kv, bottom, left, right, grad_rows, merge_weight, after,
        ),
        scratch=[
            pltpu.VMEM((KEYS, 2 * C), B16), pltpu.VMEM((KEYS, CELLS), F32),
            pltpu.VMEM((KEYS, LANES), F32), pltpu.VMEM((KEYS, LANES), F32),
            pltpu.VMEM((KEYS, LANES), B16), pltpu.VMEM((KEYS, LANES), B16),
            pltpu.VMEM((CELLS, C), B16),
        ],
        scalars=1,
        micros=9,
    )
    back_right = lax.ppermute(grad_left, LON, west)
    back_left = lax.ppermute(grad_right, LON, east)
    half = lambda rows: [((rows, 128), B16), ((rows, 128), B16)]
    grad_top, grad_own, grad_bottom = call(
        gather_kernel,
        [((EDGE, 2 * C), B16), ((CELLS, 2 * C), F32), ((EDGE, 2 * C), B16)],
        (grad_region, back_left, back_right),
    )
    from_below = lax.ppermute(grad_top, LAT, up)
    from_above = lax.ppermute(grad_bottom, LAT, down)

    mine, send, grad_mixed, grad_cross_att = call(
        mixed_kernel,
        half(ROWS_CELLS) + [((CELLS, C), F32), ((CELLS, C), B16)],
        (
            core, grad_query, grad_own, from_above, from_below, local_att, grad_rows,
            local_weight, after, cross_att, cross_weight,
        ),
        scratch=[pltpu.VMEM((2, ROWS_CELLS, 128), B16), pltpu.VMEM((CELLS, 2 * C), F32)],
        scalars=1,
        micros=3,
        loads=(6, 8, 7, 9, 10),
    )
    cells_mine, cells_partner = mine, lax.ppermute(send, "core", CORE_PAIRS)
    mine, send, grad_grid, grad_wire = call(
        cross_back_kernel,
        half(ROWS_LATE) + [((CELLS, C), F32), ((WIRE, F), B16)],
        (
            core, query, keyval, prob, grad_cross_att, grid, query_weight, sensor_weight, slots,
            grad_mixed,
        ),
        scratch=[
            pltpu.VMEM((2, ROWS_LATE, 128), B16), pltpu.VMEM((SLOTS, LANES), F32),
            pltpu.VMEM((SLOTS, LANES), B16), pltpu.VMEM((CELLS, C), B16),
            pltpu.VMEM((SLOTS, 2 * C), B16), pltpu.VMEM((GROUPS, SLOTS, LANES), B16),
            pltpu.SemaphoreType.DMA((GROUPS,)),
        ],
        scalars=1,
        micros=9,
        loads=(1, 2, 5, 6, 7, 8, 9),
        raw=(3,),
        megabytes=20,
    )
    (pair,) = call(
        sum_kernel, some(ROWS_CELLS, 1), (cells_mine, cells_partner), after=(grad_wire,)
    )
    parts = swapped_parts(pair.reshape(SIDE_COUNT, -1, 128), LAT)
    returned = lax.all_to_all(
        grad_wire.reshape(TILES, PITCH, F), ALL, split_axis=0, concat_axis=0, tiled=True
    ).reshape(WIRE, F)
    band = ROWS_CELLS // SIDE_COUNT
    thin = band // RING
    rows = ROWS_LATE // RING
    pieces = call(
        first_kernel, some(rows, RING),
        (spot("y"), mine, lax.ppermute(send, "core", CORE_PAIRS)), scalars=1,
    )
    late_parts = ring_sends("y", pieces)
    pieces = call(
        next_kernel, some(rows // RING, RING), (spot("x"), *late_parts),
        scratch=[pltpu.VMEM((rows, 128), F32)], scalars=1,
    )
    late_parts = ring_sends("x", pieces)
    (share,) = call(sum_kernel, some(rows // RING, 1), late_parts)
    bands = call(
        band_kernel, some(thin, RING), (spot("y"), parts),
        scratch=[pltpu.VMEM((band, 128), B16)], scalars=1, after=(share,),
    )
    late_parts = ring_sends(DEPTH, [share] * RING)
    (share,) = call(
        ordered_sum_kernel, some(rows // RING, 1), (spot(DEPTH), *late_parts),
        scratch=[pltpu.VMEM((RING, rows // RING, 128), F32)], scalars=1,
    )
    (inner,) = call(sum_kernel, some(thin, 1), ring_sends("y", bands), after=(share,))
    late_parts = ring_sends("x", [share] * RING)
    (share,) = call(joined_kernel, some(rows, 1), (spot("x"), *late_parts), scalars=1)
    (inner,) = call(
        sum_kernel, some(thin, 1), (inner, lax.ppermute(inner, "zhi", CORE_PAIRS)),
        after=(share,),
    )
    (grad_obs,) = call(
        return_kernel, [((OBS, F), B16)], (slot, returned), after=(inner,)
    )
    (spread,) = call(
        spread_kernel, [((SIDE_COUNT, band, 128), B16)],
        (spot("y"), *ring_sends("y", [inner] * RING)), scalars=1, after=(grad_obs,),
    )
    gathered = lax.all_to_all(spread, LAT, split_axis=0, concat_axis=0, tiled=True)
    late_parts = ring_sends("y", [share] * RING)
    (share,) = call(
        joined_kernel, some(ROWS_LATE, 1), (spot("y"), *late_parts), scalars=1, after=(spread,)
    )
    (gathered,) = call(
        hold_kernel, some(ROWS_CELLS, 1), (gathered.reshape(-1, 128),), after=(share,)
    )
    late = (share, lax.ppermute(share, "core", CORE_PAIRS))
    grad_merge, grad_local, grad_cross = call(
        unpack_cells_kernel,
        [((C, C), F32), ((C, 3 * C), F32), ((C, C), F32)],
        (core, gathered, lax.ppermute(gathered, "core", CORE_PAIRS)),
        scalars=1,
        micros=3,
    )
    grad_query_w, grad_sensor = call(
        unpack_late_kernel,
        [((C, C), F32), ((F, 2 * C), F32)],
        (core, *late),
        scalars=1,
        micros=2,
    )
    return (
        updated.reshape(TH, TW, C), grad_grid.reshape(TH, TW, C), grad_obs,
        grad_query_w, grad_sensor, grad_cross, grad_local, grad_merge,
    )


def solution(mesh):
    fine = Mesh(mesh.devices.reshape(2, 4, 4, 2, 2), ALL)
    in_specs = (
        P(LAT, LON, None), P(ALL, None), P(ALL, None), P(ALL), P(ALL),
        P(), P(), P(), P(), P(), P(LAT, LON, None),
    )
    out_specs = (P(LAT, LON, None), P(LAT, LON, None), P(ALL, None), P(), P(), P(), P(), P())
    return jax.shard_map(
        on_device, mesh=fine, in_specs=in_specs, out_specs=out_specs, check_vma=False
    )
```

```python
import math

import jax
import jax.numpy as jnp
from jax import lax
from jax.experimental import pallas as pl
from jax.experimental.pallas import tpu as pltpu
from jax.sharding import Mesh
from jax.sharding import PartitionSpec as P

B16 = jnp.bfloat16
F32 = jnp.float32
HEADS = 16
WIDTH = 32
GROUP = 4
GROUPS = HEADS // GROUP
RADIUS = 6
TH = 8
TW = 16
CELLS = TH * TW
C = 512
F = 256
OBS = 256
TILES = 128
CAP = 6
PITCH = 8
SLOTS = TILES * CAP
WIRE = TILES * PITCH
NLAT = 64
EDGE = RADIUS * TW
SIDE = 128
REGION = CELLS + 2 * EDGE
KEYS = REGION + 2 * SIDE
SCALE = 1.0 / math.sqrt(WIDTH)
LOG2E = math.log2(math.e)
LANES = GROUP * CELLS
SIDE_COUNT = 8
RING = 4
ROWS_CELLS = 5120
ROWS_LATE = 2048

ALL = ("zlo", "x", "y", "zhi", "core")
LAT = ("zlo", "x")
DEPTH = ("zlo", "zhi")
LON = ("y", "zhi", "core")
SECTOR = ("y", "zhi")


def dot(a, b):
    return jnp.dot(a, b, preferred_element_type=F32)


def dot_nt(a, b):
    return lax.dot_general(a, b, (((1,), (1,)), ((), ())), preferred_element_type=F32)


def iota(shape, dim):
    return lax.broadcasted_iota(jnp.int32, shape, dim)


def one_hot(condition):
    return jnp.where(condition, 1.0, 0.0).astype(B16)


def sixth(index):
    return lax.shift_right_logical(index * 10923, 16)


class Arriving:
    def __init__(self, source, buffer, semaphore):
        self.copy = pltpu.make_async_copy(source, buffer, semaphore)
        self.copy.start()
        self.buffer = buffer

    def __call__(self):
        self.copy.wait()
        return self.buffer


def call(
    kernel, outs, args, scratch=(), scalars=0, micros=1, after=(), loads=(), saves=(), raw=(),
    raw_outs=(), megabytes=16,
):
    vmem = pl.BlockSpec(memory_space=pltpu.VMEM)
    smem = pl.BlockSpec(memory_space=pltpu.SMEM)
    hbm = pl.BlockSpec(memory_space=pltpu.HBM)
    count, late, given, own = len(args), len(after), len(outs), len(scratch)

    def body(*refs):
        ins = list(refs[:count])
        results = list(refs[count + late : count + late + given])
        rest = refs[count + late + given :]
        held, rest = rest[:own], rest[own:]
        buffers, rest = rest[: len(loads) + len(saves)], rest[len(loads) + len(saves) :]
        semaphores = rest[0] if rest else None
        for k, i in enumerate(loads):
            ins[i] = Arriving(ins[i], buffers[k], semaphores.at[k])
        targets = list(results)
        for k, i in enumerate(saves):
            results[i] = buffers[len(loads) + k]
        kernel(*ins, *results, *held)
        leaving = [
            pltpu.make_async_copy(results[i], targets[i], semaphores.at[len(loads) + k])
            for k, i in enumerate(saves)
        ]
        for copy in leaving:
            copy.start()
        for copy in leaving:
            copy.wait()

    def spec_in(i):
        if i < scalars:
            return smem
        return hbm if i in loads or i in raw else vmem

    extra = [pltpu.VMEM(args[i].shape, args[i].dtype) for i in loads]
    extra += [pltpu.VMEM(*outs[i]) for i in saves]
    if extra:
        extra.append(pltpu.SemaphoreType.DMA((len(extra),)))
    return pl.pallas_call(
        body,
        out_shape=tuple(jax.ShapeDtypeStruct(s, d) for s, d in outs),
        in_specs=[spec_in(i) for i in range(count)]
        + [pl.BlockSpec(memory_space=pl.ANY)] * late,
        out_specs=tuple(hbm if i in saves or i in raw_outs else vmem for i in range(given)),
        scratch_shapes=list(scratch) + extra,
        compiler_params=pltpu.CompilerParams(vmem_limit_bytes=megabytes * 1024 * 1024),
        cost_estimate=pl.CostEstimate(
            flops=int(micros * 1e9), bytes_accessed=0, transcendentals=0
        ),
    )(*args, *after)


def as_column(row):
    return jnp.broadcast_to(row.astype(F32), (128, OBS)).T[:, :1].astype(jnp.int32)


def route_kernel(obs, tile_row, cell_row, accept_row, out, slot):
    trow = tile_row[...]
    tcol = as_column(trow)
    hits = jnp.where(tcol == iota((OBS, TILES), 1), 1.0, 0.0)
    before = one_hot(iota((OBS, OBS), 0) > iota((OBS, OBS), 1))
    rank_col = jnp.sum(dot(before, hits.astype(B16)) * hits, axis=1, keepdims=True).astype(jnp.int32)
    hits_t = jnp.where(trow == iota((TILES, OBS), 0), 1.0, 0.0)
    after = one_hot(iota((OBS, OBS), 0) < iota((OBS, OBS), 1))
    rank_row = jnp.sum(dot(hits_t.astype(B16), after) * hits_t, axis=0, keepdims=True).astype(jnp.int32)
    slot[...] = tcol * PITCH + rank_col
    lane = iota((OBS, F), 1)
    cell = as_column(cell_row[...])
    row_code = ((lax.shift_right_logical(cell, 4) + 1) * as_column(accept_row[...])).astype(F32)
    col_code = (cell & (TW - 1)).astype(F32)
    codes = (
        jnp.where(lane == rank_col, row_code, 0.0) + jnp.where(lane == rank_col + 8, col_code, 0.0)
    ).astype(B16)
    wire = iota((WIRE, OBS), 0)
    placed = one_hot(wire == trow * PITCH + rank_row)
    coded = one_hot(wire == trow * PITCH + CAP)
    out[...] = (dot(placed, obs[...]) + dot(coded, codes)).astype(B16)


def masked_heads(block):
    lane = lax.shift_right_logical(iota(block.shape, 1), 5)
    zero = jnp.zeros_like(block)
    return jnp.concatenate([jnp.where(lane == h, block, zero) for h in range(GROUP)], axis=0)


def head_blocks(stacked):
    return jnp.concatenate(
        [stacked[h * WIDTH : (h + 1) * WIDTH, h * CELLS : (h + 1) * CELLS] for h in range(GROUP)],
        axis=0,
    ).T


def fold(x, op):
    return op(x.reshape(x.shape[0] // 8, 8, x.shape[1]), axis=0)


def slope_of(group, h):
    return jnp.exp2(jnp.full((1, CELLS), 3.0, F32) - 0.5 * (group * GROUP + h).astype(F32))


def cross_kernel(
    arrived, grid, query_w, sensor_w, cross_w, local_w,
    keyval, query, prob, cells, local_kv,
    gap, scores,
):
    slot = iota((SLOTS, WIRE), 0)
    source = sixth(slot)
    wire = iota((SLOTS, WIRE), 1)
    rows = arrived[...]
    picked = dot(one_hot(wire == slot + 2 * source), rows).astype(B16)
    codes = dot(one_hot(wire == source * PITCH + CAP), rows[:, :128])
    keyval[:, 2 * C :] = picked
    keyval[:, : 2 * C] = dot(picked, sensor_w[...]).astype(B16)
    query[...] = dot(grid[...], query_w[...]).astype(B16)

    index = iota((SLOTS, 128), 0)
    rank = index - CAP * sixth(index)
    lane = iota((SLOTS, 128), 1)
    row_code = jnp.sum(jnp.where(lane == rank, codes, 0.0), axis=1, keepdims=True)
    col_code = jnp.sum(jnp.where(lane == rank + 8, codes, 0.0), axis=1, keepdims=True)
    cell_row = lax.shift_right_logical(lane, 4).astype(F32)
    cell_col = (lane & (TW - 1)).astype(F32)
    row_gap = (cell_row - (row_code - 1.0)) * (1.0 / TH)
    col_gap = (cell_col - col_code) * (1.0 / TW)
    gap[...] = jnp.where(row_code > 0.5, -(row_gap * row_gap + col_gap * col_gap), -1e30)

    step = 96

    def one_group(g, carry):
        lanes = pl.ds(pl.multiple_of(g * 128, 128), 128)
        values = keyval[:, pl.ds(pl.multiple_of(C + g * 128, 128), 128)]
        scores[...] = dot_nt(keyval[:, lanes], masked_heads(query[:, lanes]))
        for h in range(GROUP):
            cols = slice(h * CELLS, (h + 1) * CELLS)
            slope = slope_of(g, h) * LOG2E
            top = jnp.zeros((8, CELLS), F32)
            for r in range(0, SLOTS, step):
                s = scores[r : r + step, cols] * (SCALE * LOG2E) + slope * gap[r : r + step, :]
                scores[r : r + step, cols] = s
                top = jnp.maximum(top, fold(s, jnp.max))
            top = jnp.max(top, axis=0, keepdims=True)
            total = jnp.zeros((8, CELLS), F32)
            for r in range(0, SLOTS, step):
                e = jnp.exp2(scores[r : r + step, cols] - top)
                scores[r : r + step, cols] = e
                total = total + fold(e, jnp.sum)
            total = jnp.sum(total, axis=0, keepdims=True) + jnp.exp2(-top)
            inverse = 1.0 / total
            for r in range(0, SLOTS, step):
                prob[g, r : r + step, cols] = (scores[r : r + step, cols] * inverse).astype(B16)
        out_lanes = pl.ds(pl.multiple_of(2 * C + g * 128, 128), 128)
        cells[:, out_lanes] = head_blocks(dot(values.T, prob[g])).astype(B16)
        return carry

    lax.fori_loop(0, GROUPS, one_group, 0)
    mixed = (grid[...].astype(F32) + dot(cells[:, 2 * C :], cross_w[...])).astype(B16)
    cells[:, :C] = mixed
    qkv = dot(mixed, local_w[...]).astype(B16)
    cells[:, C : 2 * C] = qkv[:, :C]
    local_kv[...] = qkv[:, C:]


def side_rows(shape, key_dim, first_col):
    key = iota(shape, key_dim)
    line = sixth(key)
    wanted = line * TW + first_col + key - CAP * line
    return (iota(shape, 1 - key_dim) == wanted) & (key < (TH + 2 * RADIUS) * RADIUS)


def edges_kernel(top, own, bottom, left, right, kept):
    region = jnp.concatenate([top[...], own[...], bottom[...]], axis=0)
    kept[...] = region
    shape = (SIDE, REGION)
    left[...] = dot(one_hot(side_rows(shape, 0, 0)), region).astype(B16)
    right[...] = dot(one_hot(side_rows(shape, 0, TW - RADIUS)), region).astype(B16)


def window(lat_index, shape, key_row, key_col, valid):
    lane = iota(shape, 1)
    row_gap = key_row - lax.shift_right_logical(lane, 4)
    col_gap = key_col - (lane & (TW - 1))
    global_row = lat_index * TH + key_row
    seen = (jnp.abs(row_gap) <= RADIUS) & (jnp.abs(col_gap) <= RADIUS)
    seen = seen & (global_row >= 0) & (global_row < NLAT) & valid
    return jnp.where(seen, 0.0, -1e30)


def local_kernel(
    lat_index, cells, region, left, right, cotangent, merge_w,
    updated, results, grad_region, grad_left, grad_right,
    keyval, bias, scores, grad_prob, prob, grad_score, grad_att,
):
    lat = lat_index[0]
    keyval[0:REGION] = region[...]
    keyval[REGION : REGION + SIDE] = left[...]
    keyval[REGION + SIDE : KEYS] = right[...]
    grad_att[...] = dot_nt(cotangent[...], merge_w[...]).astype(B16)
    key = iota((REGION, CELLS), 0)
    bias[0:REGION] = window(
        lat, (REGION, CELLS), lax.shift_right_logical(key, 4) - RADIUS, key & (TW - 1), key >= 0
    )
    key = iota((SIDE, CELLS), 0)
    line = sixth(key)
    offset = key - CAP * line
    valid = line < TH + 2 * RADIUS
    bias[REGION : REGION + SIDE] = window(
        lat, (SIDE, CELLS), line - RADIUS, offset - RADIUS, valid
    )
    bias[REGION + SIDE : KEYS] = window(lat, (SIDE, CELLS), line - RADIUS, offset + TW, valid)

    step = 96

    def one_group(g, carry):
        lanes = pl.ds(pl.multiple_of(g * 128, 128), 128)
        upper = pl.ds(pl.multiple_of(C + g * 128, 128), 128)
        keys, values = keyval[:, lanes], keyval[:, upper]
        heads_query = masked_heads(cells[:, upper])
        heads_grad = masked_heads(grad_att[:, lanes])
        scores[...] = dot_nt(keys, heads_query)
        grad_prob[...] = dot_nt(values, heads_grad)
        for h in range(GROUP):
            cols = slice(h * CELLS, (h + 1) * CELLS)
            top_score = jnp.full((8, CELLS), -1e30, F32)
            for r in range(0, KEYS, step):
                s = scores[r : r + step, cols] * (SCALE * LOG2E) + bias[r : r + step, :]
                scores[r : r + step, cols] = s
                top_score = jnp.maximum(top_score, fold(s, jnp.max))
            top_score = jnp.max(top_score, axis=0, keepdims=True)
            total = jnp.zeros((8, CELLS), F32)
            delta = jnp.zeros((8, CELLS), F32)
            for r in range(0, KEYS, step):
                e = jnp.exp2(scores[r : r + step, cols] - top_score)
                scores[r : r + step, cols] = e
                total = total + fold(e, jnp.sum)
                delta = delta + fold(e * grad_prob[r : r + step, cols], jnp.sum)
            inverse = 1.0 / jnp.sum(total, axis=0, keepdims=True)
            delta = jnp.sum(delta, axis=0, keepdims=True) * inverse
            for r in range(0, KEYS, step):
                p = scores[r : r + step, cols] * inverse
                prob[r : r + step, cols] = p.astype(B16)
                grad_score[r : r + step, cols] = (
                    p * (grad_prob[r : r + step, cols] - delta)
                ).astype(B16)
        results[:, lanes] = head_blocks(dot(values.T, prob[...])).astype(B16)
        results[:, upper] = (head_blocks(dot(keys.T, grad_score[...])) * SCALE).astype(B16)
        grad_key = dot(grad_score[...], heads_query) * SCALE
        grad_value = dot(prob[...], heads_grad)
        for part, where_to in ((grad_key, lanes), (grad_value, upper)):
            grad_region[:, where_to] = part[0:REGION]
            grad_left[:, where_to] = part[REGION : REGION + SIDE].astype(B16)
            grad_right[:, where_to] = part[REGION + SIDE : KEYS].astype(B16)
        return carry

    lax.fori_loop(0, GROUPS, one_group, 0)
    updated[...] = (
        cells[:, :C].astype(F32) + dot(results[:, :C], merge_w[...])
    ).astype(B16)
    results[:, 2 * C : 3 * C] = cells[:, :C]
    results[:, 3 * C :] = cells[:, 2 * C :]


def gather_kernel(grad_region, from_left, from_right, top, own, bottom):
    shape = (REGION, SIDE)
    total = (
        grad_region[...]
        + dot(one_hot(side_rows(shape, 1, 0)), from_left[...])
        + dot(one_hot(side_rows(shape, 1, TW - RADIUS)), from_right[...])
    )
    top[...] = total[0:EDGE].astype(B16)
    own[...] = total[EDGE : EDGE + CELLS]
    bottom[...] = total[EDGE + CELLS : REGION].astype(B16)


def put_blocks(staged, first, product):
    height = product.shape[0]
    for i in range(product.shape[1] // 128):
        at = first + i * height
        half, row = at // staged.shape[1], at % staged.shape[1]
        staged[half, row : row + height] = product[:, i * 128 : (i + 1) * 128].astype(B16)


def split_halves(core, staged, mine, send):
    for half in range(2):

        @pl.when(core == half)
        def _(half=half):
            mine[...] = staged[half]

        @pl.when(core != half)
        def _(half=half):
            send[...] = staged[half]


def mixed_kernel(
    core_index, results, grad_kv, from_above, from_below, cotangent_in, local_in, cross_in,
    mine, send, grad_mixed, grad_cross_att,
    staged, keyval,
):
    keyval[...] = grad_kv[...]
    keyval[0:EDGE] = keyval[0:EDGE] + from_above[...].astype(F32)
    keyval[CELLS - EDGE :] = keyval[CELLS - EDGE :] + from_below[...].astype(F32)
    grad_qkv = jnp.concatenate([results[:, C : 2 * C], keyval[...].astype(B16)], axis=1)
    cotangent = cotangent_in()
    put_blocks(staged, 0, dot(results[:, :C].T, cotangent[...]))
    put_blocks(staged, 4 * C, dot(results[:, 2 * C : 3 * C].T, grad_qkv))
    mixed = cotangent[...].astype(F32) + dot_nt(grad_qkv, local_in()[...])
    grad_mixed[...] = mixed
    rounded = mixed.astype(B16)
    put_blocks(staged, 16 * C, dot(results[:, 3 * C :].T, rounded))
    grad_cross_att[...] = dot_nt(rounded, cross_in()[...]).astype(B16)
    split_halves(core_index[0], staged, mine, send)


def cross_back_kernel(
    core_index, query_in, keyval_in, prob_in, grad_att, grid, query_w, sensor_w, grad_mixed,
    mine, send, grad_grid, grad_wire,
    staged, grad_prob, grad_score, grad_query, grad_keyval, prob, prob_came,
):
    for g in range(GROUPS):
        pltpu.make_async_copy(prob_in.at[g], prob.at[g], prob_came.at[g]).start()
    query, keyval = query_in(), keyval_in()
    step = 96

    def one_group(g, carry):
        lanes = pl.ds(pl.multiple_of(g * 128, 128), 128)
        upper = pl.ds(pl.multiple_of(C + g * 128, 128), 128)
        keys, values = keyval[:, lanes], keyval[:, upper]
        heads_query = masked_heads(query[:, lanes])
        heads_grad = masked_heads(grad_att[:, lanes])
        grad_prob[...] = dot_nt(values, heads_grad)
        pltpu.make_async_copy(prob_in.at[g], prob.at[g], prob_came.at[g]).wait()
        for h in range(GROUP):
            cols = slice(h * CELLS, (h + 1) * CELLS)
            delta = jnp.zeros((8, CELLS), F32)
            for r in range(0, SLOTS, step):
                p = prob[g, r : r + step, cols].astype(F32)
                delta = delta + fold(p * grad_prob[r : r + step, cols], jnp.sum)
            delta = jnp.sum(delta, axis=0, keepdims=True)
            for r in range(0, SLOTS, step):
                p = prob[g, r : r + step, cols].astype(F32)
                grad_score[r : r + step, cols] = (
                    p * (grad_prob[r : r + step, cols] - delta)
                ).astype(B16)
        grad_query[:, lanes] = (head_blocks(dot(keys.T, grad_score[...])) * SCALE).astype(B16)
        grad_keyval[:, lanes] = (dot(grad_score[...], heads_query) * SCALE).astype(B16)
        grad_keyval[:, upper] = dot(prob[g], heads_grad).astype(B16)
        return carry

    lax.fori_loop(0, GROUPS, one_group, 0)
    grad_slots = dot_nt(grad_keyval[...], sensor_w()[...]).astype(B16)
    wire, slot = iota((WIRE, SLOTS), 0), iota((WIRE, SLOTS), 1)
    source = sixth(slot)
    grad_wire[...] = dot(one_hot(wire == slot + 2 * source), grad_slots).astype(B16)
    put_blocks(staged, 0, dot(grid()[...].T, grad_query[...]))
    put_blocks(staged, ROWS_LATE, dot(keyval[:, 2 * C :].T, grad_keyval[...]))
    grad_grid[...] = grad_mixed()[...] + dot_nt(grad_query[...], query_w()[...])
    split_halves(core_index[0], staged, mine, send)


def return_kernel(slot, returned, grad_obs):
    pick = one_hot(slot[...] == iota((OBS, WIRE), 1))
    grad_obs[...] = dot(pick, returned[...]).astype(B16)


def take_blocks(halves, first, out):
    height = out.shape[0]
    for i in range(out.shape[1] // 128):
        at = first + i * height
        half, row = at // halves[0].shape[0], at % halves[0].shape[0]
        out[:, i * 128 : (i + 1) * 128] = halves[half][row : row + height].astype(F32)


def either_core(core, pairs, write):
    for index in range(2):

        @pl.when(core == index)
        def _(index=index):
            write(*[(mine, other) if index == 0 else (other, mine) for mine, other in pairs])


def unpack_cells_kernel(core_index, mine, other, merge, local, cross):
    def write(halves):
        take_blocks(halves, 0, merge)
        take_blocks(halves, 4 * C, local)
        take_blocks(halves, 16 * C, cross)

    either_core(core_index[0], ((mine, other),), write)


def unpack_late_kernel(core_index, mine, other, query, sensor):
    def write(halves):
        take_blocks(halves, 0, query)
        take_blocks(halves, ROWS_LATE, sensor)

    either_core(core_index[0], ((mine, other),), write)


def summed_parts(parts):
    total = parts[0].astype(F32)
    for i in range(1, SIDE_COUNT):
        total = total + parts[i].astype(F32)
    return total.astype(B16)


def spread_kernel(at, *refs):
    parts, spread = refs[:RING], refs[RING]
    rows = parts[0].shape[0]
    for shift, part in enumerate(parts):
        block = part[...]
        for i in range(SIDE_COUNT):
            spread[i, chunk(ring_place(at[0], -shift), rows)] = block


def hold_kernel(block, same):
    same[...] = block[...]


def ring_place(at, shift):
    return (at + shift) & (RING - 1)


def chunk(index, rows):
    return pl.ds(pl.multiple_of(index * rows, rows), rows)


def first_kernel(at, mine, partner, *pieces):
    rows = pieces[0].shape[0]
    for shift, piece in enumerate(pieces):
        block = chunk(ring_place(at[0], shift), rows)
        piece[...] = (mine[block].astype(F32) + partner[block].astype(F32)).astype(B16)


def band_kernel(at, bands, *refs):
    pieces, band = refs[:RING], refs[RING]
    band[...] = summed_parts(bands)
    rows = pieces[0].shape[0]
    for shift, piece in enumerate(pieces):
        piece[...] = band[chunk(ring_place(at[0], shift), rows)]


def summed(parts):
    total = parts[0][...].astype(F32)
    for part in parts[1:]:
        total = total + part[...].astype(F32)
    return total


def next_kernel(at, *refs):
    parts, pieces, total = refs[:RING], refs[RING : 2 * RING], refs[-1]
    total[...] = summed(parts)
    rows = pieces[0].shape[0]
    for shift, piece in enumerate(pieces):
        piece[...] = total[chunk(ring_place(at[0], shift), rows)].astype(B16)


def sum_kernel(*refs):
    refs[-1][...] = summed(refs[:-1]).astype(B16)


def ordered_sum_kernel(at, *refs):
    parts, out, held = refs[:RING], refs[RING], refs[RING + 1]
    for shift, part in enumerate(parts):
        held[ring_place(at[0], -shift)] = part[...].astype(F32)
    out[...] = (((held[0] + held[1]) + held[2]) + held[3]).astype(B16)


def joined_kernel(at, *refs):
    parts, out = refs[:RING], refs[RING]
    rows = parts[0].shape[0]
    for shift, part in enumerate(parts):
        out[chunk(ring_place(at[0], -shift), rows)] = part[...]


def ring_sends(axis, pieces):
    return [pieces[0]] + [
        lax.ppermute(piece, axis, [(i, (i + shift) % RING) for i in range(RING)])
        for shift, piece in enumerate(pieces)
        if shift
    ]


def spot(axis):
    return lax.axis_index(axis).astype(jnp.int32).reshape(1)


def some(rows, count):
    return [((rows, 128), B16)] * count


CORE_PAIRS = ((0, 1), (1, 0))


def swapped_parts(blocks, axes):
    return lax.all_to_all(blocks, axes, split_axis=0, concat_axis=0, tiled=True)


def on_device(
    grid_state, observations, target_tile, target_cell, accepted,
    query_weight, sensor_weight, cross_weight, local_weight, merge_weight, cotangent,
):
    lat = lax.axis_index(LAT).astype(jnp.int32).reshape(1)
    core = lax.axis_index("core").astype(jnp.int32).reshape(1)
    lat_count, lon_count = NLAT // TH, TILES * TH // NLAT
    down = [(i, i + 1) for i in range(lat_count - 1)]
    up = [(i + 1, i) for i in range(lat_count - 1)]
    east = [(i, (i + 1) % lon_count) for i in range(lon_count)]
    west = [((i + 1) % lon_count, i) for i in range(lon_count)]
    grid = grid_state.reshape(CELLS, C)
    grad_rows = cotangent.reshape(CELLS, C)

    outgoing, slot = call(
        route_kernel,
        [((WIRE, F), B16), ((OBS, 1), jnp.int32)],
        (
            observations, target_tile.reshape(1, OBS), target_cell.reshape(1, OBS),
            accepted.reshape(1, OBS),
        ),
    )
    arrived = lax.all_to_all(
        outgoing.reshape(TILES, PITCH, F), ALL, split_axis=0, concat_axis=0, tiled=True
    ).reshape(WIRE, F)

    keyval, query, prob, cells, local_kv = call(
        cross_kernel,
        [
            ((SLOTS, 2 * C + F), B16), ((CELLS, C), B16),
            ((GROUPS, SLOTS, LANES), B16), ((CELLS, 3 * C), B16), ((CELLS, 2 * C), B16),
        ],
        (arrived, grid, query_weight, sensor_weight, cross_weight, local_weight),
        scratch=[pltpu.VMEM((SLOTS, CELLS), F32), pltpu.VMEM((SLOTS, LANES), F32)],
        micros=7,
    )

    top = lax.ppermute(local_kv[CELLS - EDGE :], LAT, down)
    bottom = lax.ppermute(local_kv[:EDGE], LAT, up)
    send_left, send_right, region = call(
        edges_kernel,
        [((SIDE, 2 * C), B16), ((SIDE, 2 * C), B16), ((REGION, 2 * C), B16)],
        (top, local_kv, bottom),
    )
    left = lax.ppermute(send_right, LON, east)
    right = lax.ppermute(send_left, LON, west)

    updated, results, grad_region, grad_left, grad_right = call(
        local_kernel,
        [
            ((CELLS, C), B16), ((CELLS, 4 * C), B16),
            ((REGION, 2 * C), F32), ((SIDE, 2 * C), B16), ((SIDE, 2 * C), B16),
        ],
        (
            lat, cells, region, left, right, grad_rows, merge_weight,
        ),
        scratch=[
            pltpu.VMEM((KEYS, 2 * C), B16), pltpu.VMEM((KEYS, CELLS), F32),
            pltpu.VMEM((KEYS, LANES), F32), pltpu.VMEM((KEYS, LANES), F32),
            pltpu.VMEM((KEYS, LANES), B16), pltpu.VMEM((KEYS, LANES), B16),
            pltpu.VMEM((CELLS, C), B16),
        ],
        scalars=1,
        micros=9,
    )
    back_right = lax.ppermute(grad_left, LON, west)
    back_left = lax.ppermute(grad_right, LON, east)
    half = lambda rows: [((rows, 128), B16), ((rows, 128), B16)]
    grad_top, grad_own, grad_bottom = call(
        gather_kernel,
        [((EDGE, 2 * C), B16), ((CELLS, 2 * C), F32), ((EDGE, 2 * C), B16)],
        (grad_region, back_left, back_right),
    )
    from_below = lax.ppermute(grad_top, LAT, up)
    from_above = lax.ppermute(grad_bottom, LAT, down)

    mine, send, grad_mixed, grad_cross_att = call(
        mixed_kernel,
        half(ROWS_CELLS) + [((CELLS, C), F32), ((CELLS, C), B16)],
        (
            core, results, grad_own, from_above, from_below, grad_rows, local_weight,
            cross_weight,
        ),
        scratch=[pltpu.VMEM((2, ROWS_CELLS, 128), B16), pltpu.VMEM((CELLS, 2 * C), F32)],
        scalars=1,
        micros=3,
        loads=(5, 6, 7),
    )
    cells_mine, cells_partner = mine, lax.ppermute(send, "core", CORE_PAIRS)
    mine, send, grad_grid, grad_wire = call(
        cross_back_kernel,
        half(ROWS_LATE) + [((CELLS, C), F32), ((WIRE, F), B16)],
        (
            core, query, keyval, prob, grad_cross_att, grid, query_weight, sensor_weight,
            grad_mixed,
        ),
        scratch=[
            pltpu.VMEM((2, ROWS_LATE, 128), B16), pltpu.VMEM((SLOTS, LANES), F32),
            pltpu.VMEM((SLOTS, LANES), B16), pltpu.VMEM((CELLS, C), B16),
            pltpu.VMEM((SLOTS, 2 * C), B16), pltpu.VMEM((GROUPS, SLOTS, LANES), B16),
            pltpu.SemaphoreType.DMA((GROUPS,)),
        ],
        scalars=1,
        micros=9,
        loads=(1, 2, 5, 6, 7, 8),
        raw=(3,),
        megabytes=20,
    )
    (pair,) = call(
        sum_kernel, some(ROWS_CELLS, 1), (cells_mine, cells_partner), after=(grad_wire,)
    )
    parts = swapped_parts(pair.reshape(SIDE_COUNT, -1, 128), LAT)
    returned = lax.all_to_all(
        grad_wire.reshape(TILES, PITCH, F), ALL, split_axis=0, concat_axis=0, tiled=True
    ).reshape(WIRE, F)
    band = ROWS_CELLS // SIDE_COUNT
    thin = band // RING
    rows = ROWS_LATE // RING
    pieces = call(
        first_kernel, some(rows, RING),
        (spot("y"), mine, lax.ppermute(send, "core", CORE_PAIRS)), scalars=1,
    )
    late_parts = ring_sends("y", pieces)
    pieces = call(
        next_kernel, some(rows // RING, RING), (spot("x"), *late_parts),
        scratch=[pltpu.VMEM((rows, 128), F32)], scalars=1,
    )
    late_parts = ring_sends("x", pieces)
    (share,) = call(sum_kernel, some(rows // RING, 1), late_parts)
    bands = call(
        band_kernel, some(thin, RING), (spot("y"), parts),
        scratch=[pltpu.VMEM((band, 128), B16)], scalars=1, after=(share,),
    )
    late_parts = ring_sends(DEPTH, [share] * RING)
    (share,) = call(
        ordered_sum_kernel, some(rows // RING, 1), (spot(DEPTH), *late_parts),
        scratch=[pltpu.VMEM((RING, rows // RING, 128), F32)], scalars=1,
    )
    (inner,) = call(sum_kernel, some(thin, 1), ring_sends("y", bands), after=(share,))
    late_parts = ring_sends("x", [share] * RING)
    (share,) = call(joined_kernel, some(rows, 1), (spot("x"), *late_parts), scalars=1)
    (inner,) = call(
        sum_kernel, some(thin, 1), (inner, lax.ppermute(inner, "zhi", CORE_PAIRS)),
        after=(share,),
    )
    (grad_obs,) = call(
        return_kernel, [((OBS, F), B16)], (slot, returned), after=(inner,)
    )
    (spread,) = call(
        spread_kernel, [((SIDE_COUNT, band, 128), B16)],
        (spot("y"), *ring_sends("y", [inner] * RING)), scalars=1, after=(grad_obs,),
    )
    gathered = lax.all_to_all(spread, LAT, split_axis=0, concat_axis=0, tiled=True)
    late_parts = ring_sends("y", [share] * RING)
    (share,) = call(
        joined_kernel, some(ROWS_LATE, 1), (spot("y"), *late_parts), scalars=1, after=(spread,)
    )
    (gathered,) = call(
        hold_kernel, some(ROWS_CELLS, 1), (gathered.reshape(-1, 128),), after=(share,)
    )
    late = (share, lax.ppermute(share, "core", CORE_PAIRS))
    grad_merge, grad_local, grad_cross = call(
        unpack_cells_kernel,
        [((C, C), F32), ((C, 3 * C), F32), ((C, C), F32)],
        (core, gathered, lax.ppermute(gathered, "core", CORE_PAIRS)),
        scalars=1,
        micros=3,
    )
    grad_query_w, grad_sensor = call(
        unpack_late_kernel,
        [((C, C), F32), ((F, 2 * C), F32)],
        (core, *late),
        scalars=1,
        micros=2,
    )
    return (
        updated.reshape(TH, TW, C), grad_grid.reshape(TH, TW, C), grad_obs,
        grad_query_w, grad_sensor, grad_cross, grad_local, grad_merge,
    )


def solution(mesh):
    fine = Mesh(mesh.devices.reshape(2, 4, 4, 2, 2), ALL)
    in_specs = (
        P(LAT, LON, None), P(ALL, None), P(ALL, None), P(ALL), P(ALL),
        P(), P(), P(), P(), P(), P(LAT, LON, None),
    )
    out_specs = (P(LAT, LON, None), P(LAT, LON, None), P(ALL, None), P(), P(), P(), P(), P())
    return jax.shard_map(
        on_device, mesh=fine, in_specs=in_specs, out_specs=out_specs, check_vma=False
    )
```

```python
import math

import jax
import jax.numpy as jnp
from jax import lax
from jax.experimental import pallas as pl
from jax.experimental.pallas import tpu as pltpu
from jax.sharding import Mesh
from jax.sharding import PartitionSpec as P

B16 = jnp.bfloat16
F32 = jnp.float32
HEADS = 16
WIDTH = 32
GROUP = 4
GROUPS = HEADS // GROUP
RADIUS = 6
TH = 8
TW = 16
CELLS = TH * TW
C = 512
F = 256
OBS = 256
TILES = 128
CAP = 6
PITCH = 8
SLOTS = TILES * CAP
WIRE = TILES * PITCH
NLAT = 64
EDGE = RADIUS * TW
SIDE = 128
REGION = CELLS + 2 * EDGE
KEYS = REGION + 2 * SIDE
SCALE = 1.0 / math.sqrt(WIDTH)
LOG2E = math.log2(math.e)
LANES = GROUP * CELLS
SIDE_COUNT = 8
RING = 4
ROWS_CELLS = 5120
ROWS_LATE = 2048

ALL = ("zlo", "x", "y", "zhi", "core")
LAT = ("zlo", "x")
DEPTH = ("zlo", "zhi")
LON = ("y", "zhi", "core")
SECTOR = ("y", "zhi")


def dot(a, b):
    return jnp.dot(a, b, preferred_element_type=F32)


def dot_nt(a, b):
    return lax.dot_general(a, b, (((1,), (1,)), ((), ())), preferred_element_type=F32)


def iota(shape, dim):
    return lax.broadcasted_iota(jnp.int32, shape, dim)


def one_hot(condition):
    return jnp.where(condition, 1.0, 0.0).astype(B16)


def sixth(index):
    return lax.shift_right_logical(index * 10923, 16)


class Arriving:
    def __init__(self, source, buffer, semaphore):
        self.copy = pltpu.make_async_copy(source, buffer, semaphore)
        self.copy.start()
        self.buffer = buffer

    def __call__(self):
        self.copy.wait()
        return self.buffer


def call(
    kernel, outs, args, scratch=(), scalars=0, micros=1, after=(), loads=(), saves=(), raw=(),
    raw_outs=(), megabytes=16,
):
    vmem = pl.BlockSpec(memory_space=pltpu.VMEM)
    smem = pl.BlockSpec(memory_space=pltpu.SMEM)
    hbm = pl.BlockSpec(memory_space=pltpu.HBM)
    count, late, given, own = len(args), len(after), len(outs), len(scratch)

    def body(*refs):
        ins = list(refs[:count])
        results = list(refs[count + late : count + late + given])
        rest = refs[count + late + given :]
        held, rest = rest[:own], rest[own:]
        buffers, rest = rest[: len(loads) + len(saves)], rest[len(loads) + len(saves) :]
        semaphores = rest[0] if rest else None
        for k, i in enumerate(loads):
            ins[i] = Arriving(ins[i], buffers[k], semaphores.at[k])
        targets = list(results)
        for k, i in enumerate(saves):
            results[i] = buffers[len(loads) + k]
        kernel(*ins, *results, *held)
        leaving = [
            pltpu.make_async_copy(results[i], targets[i], semaphores.at[len(loads) + k])
            for k, i in enumerate(saves)
        ]
        for copy in leaving:
            copy.start()
        for copy in leaving:
            copy.wait()

    def spec_in(i):
        if i < scalars:
            return smem
        return hbm if i in loads or i in raw else vmem

    extra = [pltpu.VMEM(args[i].shape, args[i].dtype) for i in loads]
    extra += [pltpu.VMEM(*outs[i]) for i in saves]
    if extra:
        extra.append(pltpu.SemaphoreType.DMA((len(extra),)))
    return pl.pallas_call(
        body,
        out_shape=tuple(jax.ShapeDtypeStruct(s, d) for s, d in outs),
        in_specs=[spec_in(i) for i in range(count)]
        + [pl.BlockSpec(memory_space=pl.ANY)] * late,
        out_specs=tuple(hbm if i in saves or i in raw_outs else vmem for i in range(given)),
        scratch_shapes=list(scratch) + extra,
        compiler_params=pltpu.CompilerParams(vmem_limit_bytes=megabytes * 1024 * 1024),
        cost_estimate=pl.CostEstimate(
            flops=int(micros * 1e9), bytes_accessed=0, transcendentals=0
        ),
    )(*args, *after)


def as_column(row):
    return jnp.broadcast_to(row.astype(F32), (128, OBS)).T[:, :1].astype(jnp.int32)


def route_kernel(obs, marks, out, slot):
    trow = marks[0:1]
    tcol = as_column(trow)
    hits = jnp.where(tcol == iota((OBS, TILES), 1), 1.0, 0.0)
    before = one_hot(iota((OBS, OBS), 0) > iota((OBS, OBS), 1))
    rank_col = jnp.sum(dot(before, hits.astype(B16)) * hits, axis=1, keepdims=True).astype(jnp.int32)
    hits_t = jnp.where(trow == iota((TILES, OBS), 0), 1.0, 0.0)
    after = one_hot(iota((OBS, OBS), 0) < iota((OBS, OBS), 1))
    rank_row = jnp.sum(dot(hits_t.astype(B16), after) * hits_t, axis=0, keepdims=True).astype(jnp.int32)
    slot[...] = tcol * PITCH + rank_col
    lane = iota((OBS, F), 1)
    cell = as_column(marks[1:2])
    row_code = ((lax.shift_right_logical(cell, 4) + 1) * as_column(marks[2:3])).astype(F32)
    col_code = (cell & (TW - 1)).astype(F32)
    codes = (
        jnp.where(lane == rank_col, row_code, 0.0) + jnp.where(lane == rank_col + 8, col_code, 0.0)
    ).astype(B16)
    wire = iota((WIRE, OBS), 0)
    placed = one_hot(wire == trow * PITCH + rank_row)
    coded = one_hot(wire == trow * PITCH + CAP)
    out[...] = (dot(placed, obs[...]) + dot(coded, codes)).astype(B16)


def masked_heads(block):
    lane = lax.shift_right_logical(iota(block.shape, 1), 5)
    zero = jnp.zeros_like(block)
    return jnp.concatenate([jnp.where(lane == h, block, zero) for h in range(GROUP)], axis=0)


def head_blocks(stacked):
    return jnp.concatenate(
        [stacked[h * WIDTH : (h + 1) * WIDTH, h * CELLS : (h + 1) * CELLS] for h in range(GROUP)],
        axis=0,
    ).T


def fold(x, op):
    return op(x.reshape(x.shape[0] // 8, 8, x.shape[1]), axis=0)


def slope_of(group, h):
    return jnp.exp2(jnp.full((1, CELLS), 3.0, F32) - 0.5 * (group * GROUP + h).astype(F32))


def cross_kernel(
    arrived, grid, query_w, sensor_w, cross_w, local_w,
    keyval, query, prob, cells, local_kv,
    gap, scores,
):
    slot = iota((SLOTS, WIRE), 0)
    source = sixth(slot)
    wire = iota((SLOTS, WIRE), 1)
    rows = arrived[...]
    picked = dot(one_hot(wire == slot + 2 * source), rows).astype(B16)
    codes = dot(one_hot(wire == source * PITCH + CAP), rows[:, :128])
    keyval[:, 2 * C :] = picked
    keyval[:, : 2 * C] = dot(picked, sensor_w[...]).astype(B16)
    query[...] = dot(grid[...], query_w[...]).astype(B16)

    index = iota((SLOTS, 128), 0)
    rank = index - CAP * sixth(index)
    lane = iota((SLOTS, 128), 1)
    row_code = jnp.sum(jnp.where(lane == rank, codes, 0.0), axis=1, keepdims=True)
    col_code = jnp.sum(jnp.where(lane == rank + 8, codes, 0.0), axis=1, keepdims=True)
    cell_row = lax.shift_right_logical(lane, 4).astype(F32)
    cell_col = (lane & (TW - 1)).astype(F32)
    row_gap = (cell_row - (row_code - 1.0)) * (1.0 / TH)
    col_gap = (cell_col - col_code) * (1.0 / TW)
    gap[...] = jnp.where(row_code > 0.5, -(row_gap * row_gap + col_gap * col_gap), -1e30)

    step = 96

    def one_group(g, carry):
        lanes = pl.ds(pl.multiple_of(g * 128, 128), 128)
        values = keyval[:, pl.ds(pl.multiple_of(C + g * 128, 128), 128)]
        scores[...] = dot_nt(keyval[:, lanes], masked_heads(query[:, lanes]))
        for h in range(GROUP):
            cols = slice(h * CELLS, (h + 1) * CELLS)
            slope = slope_of(g, h) * LOG2E
            top = jnp.zeros((8, CELLS), F32)
            for r in range(0, SLOTS, step):
                s = scores[r : r + step, cols] * (SCALE * LOG2E) + slope * gap[r : r + step, :]
                scores[r : r + step, cols] = s
                top = jnp.maximum(top, fold(s, jnp.max))
            top = jnp.max(top, axis=0, keepdims=True)
            total = jnp.zeros((8, CELLS), F32)
            for r in range(0, SLOTS, step):
                e = jnp.exp2(scores[r : r + step, cols] - top)
                scores[r : r + step, cols] = e
                total = total + fold(e, jnp.sum)
            total = jnp.sum(total, axis=0, keepdims=True) + jnp.exp2(-top)
            inverse = 1.0 / total
            for r in range(0, SLOTS, step):
                prob[g, r : r + step, cols] = (scores[r : r + step, cols] * inverse).astype(B16)
        out_lanes = pl.ds(pl.multiple_of(2 * C + g * 128, 128), 128)
        cells[:, out_lanes] = head_blocks(dot(values.T, prob[g])).astype(B16)
        return carry

    lax.fori_loop(0, GROUPS, one_group, 0)
    mixed = (grid[...].astype(F32) + dot(cells[:, 2 * C :], cross_w[...])).astype(B16)
    cells[:, :C] = mixed
    qkv = dot(mixed, local_w[...]).astype(B16)
    cells[:, C : 2 * C] = qkv[:, :C]
    local_kv[...] = qkv[:, C:]


def side_rows(shape, key_dim, first_col):
    key = iota(shape, key_dim)
    line = sixth(key)
    wanted = line * TW + first_col + key - CAP * line
    return (iota(shape, 1 - key_dim) == wanted) & (key < (TH + 2 * RADIUS) * RADIUS)


def edges_kernel(top, own, bottom, left, right, kept):
    region = jnp.concatenate([top[...], own[...], bottom[...]], axis=0)
    kept[...] = region
    shape = (SIDE, REGION)
    left[...] = dot(one_hot(side_rows(shape, 0, 0)), region).astype(B16)
    right[...] = dot(one_hot(side_rows(shape, 0, TW - RADIUS)), region).astype(B16)


def window(lat_index, shape, key_row, key_col, valid):
    lane = iota(shape, 1)
    row_gap = key_row - lax.shift_right_logical(lane, 4)
    col_gap = key_col - (lane & (TW - 1))
    global_row = lat_index * TH + key_row
    seen = (jnp.abs(row_gap) <= RADIUS) & (jnp.abs(col_gap) <= RADIUS)
    seen = seen & (global_row >= 0) & (global_row < NLAT) & valid
    return jnp.where(seen, 0.0, -1e30)


def local_kernel(
    lat_index, cells, region, left, right, cotangent, merge_w,
    updated, results, grad_region, grad_left, grad_right,
    keyval, bias, scores, grad_prob, prob, grad_score, grad_att,
):
    lat = lat_index[0]
    keyval[0:REGION] = region[...]
    keyval[REGION : REGION + SIDE] = left[...]
    keyval[REGION + SIDE : KEYS] = right[...]
    grad_att[...] = dot_nt(cotangent[...], merge_w[...]).astype(B16)
    key = iota((REGION, CELLS), 0)
    bias[0:REGION] = window(
        lat, (REGION, CELLS), lax.shift_right_logical(key, 4) - RADIUS, key & (TW - 1), key >= 0
    )
    key = iota((SIDE, CELLS), 0)
    line = sixth(key)
    offset = key - CAP * line
    valid = line < TH + 2 * RADIUS
    bias[REGION : REGION + SIDE] = window(
        lat, (SIDE, CELLS), line - RADIUS, offset - RADIUS, valid
    )
    bias[REGION + SIDE : KEYS] = window(lat, (SIDE, CELLS), line - RADIUS, offset + TW, valid)

    step = 96

    def one_group(g, carry):
        lanes = pl.ds(pl.multiple_of(g * 128, 128), 128)
        upper = pl.ds(pl.multiple_of(C + g * 128, 128), 128)
        keys, values = keyval[:, lanes], keyval[:, upper]
        heads_query = masked_heads(cells[:, upper])
        heads_grad = masked_heads(grad_att[:, lanes])
        scores[...] = dot_nt(keys, heads_query)
        grad_prob[...] = dot_nt(values, heads_grad)
        for h in range(GROUP):
            cols = slice(h * CELLS, (h + 1) * CELLS)
            top_score = jnp.full((8, CELLS), -1e30, F32)
            for r in range(0, KEYS, step):
                s = scores[r : r + step, cols] * (SCALE * LOG2E) + bias[r : r + step, :]
                scores[r : r + step, cols] = s
                top_score = jnp.maximum(top_score, fold(s, jnp.max))
            top_score = jnp.max(top_score, axis=0, keepdims=True)
            total = jnp.zeros((8, CELLS), F32)
            delta = jnp.zeros((8, CELLS), F32)
            for r in range(0, KEYS, step):
                e = jnp.exp2(scores[r : r + step, cols] - top_score)
                scores[r : r + step, cols] = e
                total = total + fold(e, jnp.sum)
                delta = delta + fold(e * grad_prob[r : r + step, cols], jnp.sum)
            inverse = 1.0 / jnp.sum(total, axis=0, keepdims=True)
            delta = jnp.sum(delta, axis=0, keepdims=True) * inverse
            for r in range(0, KEYS, step):
                p = scores[r : r + step, cols] * inverse
                prob[r : r + step, cols] = p.astype(B16)
                grad_score[r : r + step, cols] = (
                    p * (grad_prob[r : r + step, cols] - delta)
                ).astype(B16)
        results[:, lanes] = head_blocks(dot(values.T, prob[...])).astype(B16)
        results[:, upper] = (head_blocks(dot(keys.T, grad_score[...])) * SCALE).astype(B16)
        grad_key = dot(grad_score[...], heads_query) * SCALE
        grad_value = dot(prob[...], heads_grad)
        for part, where_to in ((grad_key, lanes), (grad_value, upper)):
            grad_region[:, where_to] = part[0:REGION]
            grad_left[:, where_to] = part[REGION : REGION + SIDE].astype(B16)
            grad_right[:, where_to] = part[REGION + SIDE : KEYS].astype(B16)
        return carry

    lax.fori_loop(0, GROUPS, one_group, 0)
    updated[...] = (
        cells[:, :C].astype(F32) + dot(results[:, :C], merge_w[...])
    ).astype(B16)
    results[:, 2 * C : 3 * C] = cells[:, :C]
    results[:, 3 * C :] = cells[:, 2 * C :]


def gather_kernel(grad_region, from_left, from_right, top, own, bottom):
    shape = (REGION, SIDE)
    total = (
        grad_region[...]
        + dot(one_hot(side_rows(shape, 1, 0)), from_left[...])
        + dot(one_hot(side_rows(shape, 1, TW - RADIUS)), from_right[...])
    )
    top[...] = total[0:EDGE].astype(B16)
    own[...] = total[EDGE : EDGE + CELLS]
    bottom[...] = total[EDGE + CELLS : REGION].astype(B16)


def put_blocks(staged, first, product):
    height = product.shape[0]
    for i in range(product.shape[1] // 128):
        at = first + i * height
        half, row = at // staged.shape[1], at % staged.shape[1]
        staged[half, row : row + height] = product[:, i * 128 : (i + 1) * 128].astype(B16)


def split_halves(core, staged, mine, send):
    for half in range(2):

        @pl.when(core == half)
        def _(half=half):
            mine[...] = staged[half]

        @pl.when(core != half)
        def _(half=half):
            send[...] = staged[half]


def mixed_kernel(
    core_index, results, grad_kv, from_above, from_below, cotangent_in, local_in, cross_in,
    mine, send, grad_mixed, grad_cross_att,
    staged, keyval,
):
    keyval[...] = grad_kv[...]
    keyval[0:EDGE] = keyval[0:EDGE] + from_above[...].astype(F32)
    keyval[CELLS - EDGE :] = keyval[CELLS - EDGE :] + from_below[...].astype(F32)
    grad_qkv = jnp.concatenate([results[:, C : 2 * C], keyval[...].astype(B16)], axis=1)
    cotangent = cotangent_in()
    put_blocks(staged, 0, dot(results[:, :C].T, cotangent[...]))
    put_blocks(staged, 4 * C, dot(results[:, 2 * C : 3 * C].T, grad_qkv))
    mixed = cotangent[...].astype(F32) + dot_nt(grad_qkv, local_in()[...])
    grad_mixed[...] = mixed
    rounded = mixed.astype(B16)
    put_blocks(staged, 16 * C, dot(results[:, 3 * C :].T, rounded))
    grad_cross_att[...] = dot_nt(rounded, cross_in()[...]).astype(B16)
    split_halves(core_index[0], staged, mine, send)


def cross_back_kernel(
    core_index, query_in, keyval_in, prob_in, grad_att, grid, query_w, sensor_w, grad_mixed,
    mine, send, grad_grid, grad_wire,
    staged, grad_prob, grad_score, grad_query, grad_keyval, prob, prob_came,
):
    for g in range(GROUPS):
        pltpu.make_async_copy(prob_in.at[g], prob.at[g], prob_came.at[g]).start()
    query, keyval = query_in(), keyval_in()
    step = 96

    def one_group(g, carry):
        lanes = pl.ds(pl.multiple_of(g * 128, 128), 128)
        upper = pl.ds(pl.multiple_of(C + g * 128, 128), 128)
        keys, values = keyval[:, lanes], keyval[:, upper]
        heads_query = masked_heads(query[:, lanes])
        heads_grad = masked_heads(grad_att[:, lanes])
        grad_prob[...] = dot_nt(values, heads_grad)
        pltpu.make_async_copy(prob_in.at[g], prob.at[g], prob_came.at[g]).wait()
        for h in range(GROUP):
            cols = slice(h * CELLS, (h + 1) * CELLS)
            delta = jnp.zeros((8, CELLS), F32)
            for r in range(0, SLOTS, step):
                p = prob[g, r : r + step, cols].astype(F32)
                delta = delta + fold(p * grad_prob[r : r + step, cols], jnp.sum)
            delta = jnp.sum(delta, axis=0, keepdims=True)
            for r in range(0, SLOTS, step):
                p = prob[g, r : r + step, cols].astype(F32)
                grad_score[r : r + step, cols] = (
                    p * (grad_prob[r : r + step, cols] - delta)
                ).astype(B16)
        grad_query[:, lanes] = (head_blocks(dot(keys.T, grad_score[...])) * SCALE).astype(B16)
        grad_keyval[:, lanes] = (dot(grad_score[...], heads_query) * SCALE).astype(B16)
        grad_keyval[:, upper] = dot(prob[g], heads_grad).astype(B16)
        return carry

    lax.fori_loop(0, GROUPS, one_group, 0)
    grad_slots = dot_nt(grad_keyval[...], sensor_w()[...]).astype(B16)
    wire, slot = iota((WIRE, SLOTS), 0), iota((WIRE, SLOTS), 1)
    source = sixth(slot)
    grad_wire[...] = dot(one_hot(wire == slot + 2 * source), grad_slots).astype(B16)
    put_blocks(staged, 0, dot(grid()[...].T, grad_query[...]))
    put_blocks(staged, ROWS_LATE, dot(keyval[:, 2 * C :].T, grad_keyval[...]))
    grad_grid[...] = grad_mixed()[...] + dot_nt(grad_query[...], query_w()[...])
    split_halves(core_index[0], staged, mine, send)


def return_kernel(slot, returned, grad_obs):
    pick = one_hot(slot[...] == iota((OBS, WIRE), 1))
    grad_obs[...] = dot(pick, returned[...]).astype(B16)


def take_blocks(halves, first, out):
    height = out.shape[0]
    for i in range(out.shape[1] // 128):
        at = first + i * height
        half, row = at // halves[0].shape[0], at % halves[0].shape[0]
        out[:, i * 128 : (i + 1) * 128] = halves[half][row : row + height].astype(F32)


def either_core(core, pairs, write):
    for index in range(2):

        @pl.when(core == index)
        def _(index=index):
            write(*[(mine, other) if index == 0 else (other, mine) for mine, other in pairs])


def unpack_cells_kernel(core_index, mine, other, merge, local, cross):
    def write(halves):
        take_blocks(halves, 0, merge)
        take_blocks(halves, 4 * C, local)
        take_blocks(halves, 16 * C, cross)

    either_core(core_index[0], ((mine, other),), write)


def unpack_late_kernel(core_index, mine, other, query, sensor):
    def write(halves):
        take_blocks(halves, 0, query)
        take_blocks(halves, ROWS_LATE, sensor)

    either_core(core_index[0], ((mine, other),), write)


def summed_parts(parts):
    total = parts[0].astype(F32)
    for i in range(1, SIDE_COUNT):
        total = total + parts[i].astype(F32)
    return total.astype(B16)


def spread_kernel(at, *refs):
    parts, spread = refs[:RING], refs[RING]
    rows = parts[0].shape[0]
    for shift, part in enumerate(parts):
        block = part[...]
        for i in range(SIDE_COUNT):
            spread[i, chunk(ring_place(at[0], -shift), rows)] = block


def hold_kernel(block, same):
    same[...] = block[...]


def ring_place(at, shift):
    return (at + shift) & (RING - 1)


def chunk(index, rows):
    return pl.ds(pl.multiple_of(index * rows, rows), rows)


def first_kernel(at, mine, partner, *pieces):
    rows = pieces[0].shape[0]
    for shift, piece in enumerate(pieces):
        block = chunk(ring_place(at[0], shift), rows)
        piece[...] = (mine[block].astype(F32) + partner[block].astype(F32)).astype(B16)


def band_kernel(at, bands, *refs):
    pieces, band = refs[:RING], refs[RING]
    band[...] = summed_parts(bands)
    rows = pieces[0].shape[0]
    for shift, piece in enumerate(pieces):
        piece[...] = band[chunk(ring_place(at[0], shift), rows)]


def summed(parts):
    total = parts[0][...].astype(F32)
    for part in parts[1:]:
        total = total + part[...].astype(F32)
    return total


def next_kernel(at, *refs):
    parts, pieces, total = refs[:RING], refs[RING : 2 * RING], refs[-1]
    total[...] = summed(parts)
    rows = pieces[0].shape[0]
    for shift, piece in enumerate(pieces):
        piece[...] = total[chunk(ring_place(at[0], shift), rows)].astype(B16)


def sum_kernel(*refs):
    refs[-1][...] = summed(refs[:-1]).astype(B16)


def ordered_sum_kernel(at, *refs):
    parts, out, held = refs[:RING], refs[RING], refs[RING + 1]
    for shift, part in enumerate(parts):
        held[ring_place(at[0], -shift)] = part[...].astype(F32)
    out[...] = (((held[0] + held[1]) + held[2]) + held[3]).astype(B16)


def joined_kernel(at, *refs):
    parts, out = refs[:RING], refs[RING]
    rows = parts[0].shape[0]
    for shift, part in enumerate(parts):
        out[chunk(ring_place(at[0], -shift), rows)] = part[...]


def ring_sends(axis, pieces):
    return [pieces[0]] + [
        lax.ppermute(piece, axis, [(i, (i + shift) % RING) for i in range(RING)])
        for shift, piece in enumerate(pieces)
        if shift
    ]


def spot(axis):
    return lax.axis_index(axis).astype(jnp.int32).reshape(1)


def some(rows, count):
    return [((rows, 128), B16)] * count


CORE_PAIRS = ((0, 1), (1, 0))


def swapped_parts(blocks, axes):
    return lax.all_to_all(blocks, axes, split_axis=0, concat_axis=0, tiled=True)


def on_device(
    grid_state, observations, target_tile, target_cell, accepted,
    query_weight, sensor_weight, cross_weight, local_weight, merge_weight, cotangent,
):
    lat = lax.axis_index(LAT).astype(jnp.int32).reshape(1)
    core = lax.axis_index("core").astype(jnp.int32).reshape(1)
    lat_count, lon_count = NLAT // TH, TILES * TH // NLAT
    down = [(i, i + 1) for i in range(lat_count - 1)]
    up = [(i + 1, i) for i in range(lat_count - 1)]
    east = [(i, (i + 1) % lon_count) for i in range(lon_count)]
    west = [((i + 1) % lon_count, i) for i in range(lon_count)]
    grid = grid_state.reshape(CELLS, C)
    grad_rows = cotangent.reshape(CELLS, C)

    outgoing, slot = call(
        route_kernel,
        [((WIRE, F), B16), ((OBS, 1), jnp.int32)],
        (
            observations, jnp.stack([target_tile[:, 0], target_cell, accepted]),
        ),
    )
    arrived = lax.all_to_all(
        outgoing.reshape(TILES, PITCH, F), ALL, split_axis=0, concat_axis=0, tiled=True
    ).reshape(WIRE, F)

    keyval, query, prob, cells, local_kv = call(
        cross_kernel,
        [
            ((SLOTS, 2 * C + F), B16), ((CELLS, C), B16),
            ((GROUPS, SLOTS, LANES), B16), ((CELLS, 3 * C), B16), ((CELLS, 2 * C), B16),
        ],
        (arrived, grid, query_weight, sensor_weight, cross_weight, local_weight),
        scratch=[pltpu.VMEM((SLOTS, CELLS), F32), pltpu.VMEM((SLOTS, LANES), F32)],
        micros=7,
    )

    top = lax.ppermute(local_kv[CELLS - EDGE :], LAT, down)
    bottom = lax.ppermute(local_kv[:EDGE], LAT, up)
    send_left, send_right, region = call(
        edges_kernel,
        [((SIDE, 2 * C), B16), ((SIDE, 2 * C), B16), ((REGION, 2 * C), B16)],
        (top, local_kv, bottom),
    )
    left = lax.ppermute(send_right, LON, east)
    right = lax.ppermute(send_left, LON, west)

    updated, results, grad_region, grad_left, grad_right = call(
        local_kernel,
        [
            ((CELLS, C), B16), ((CELLS, 4 * C), B16),
            ((REGION, 2 * C), F32), ((SIDE, 2 * C), B16), ((SIDE, 2 * C), B16),
        ],
        (
            lat, cells, region, left, right, grad_rows, merge_weight,
        ),
        scratch=[
            pltpu.VMEM((KEYS, 2 * C), B16), pltpu.VMEM((KEYS, CELLS), F32),
            pltpu.VMEM((KEYS, LANES), F32), pltpu.VMEM((KEYS, LANES), F32),
            pltpu.VMEM((KEYS, LANES), B16), pltpu.VMEM((KEYS, LANES), B16),
            pltpu.VMEM((CELLS, C), B16),
        ],
        scalars=1,
        micros=9,
    )
    back_right = lax.ppermute(grad_left, LON, west)
    back_left = lax.ppermute(grad_right, LON, east)
    half = lambda rows: [((rows, 128), B16), ((rows, 128), B16)]
    grad_top, grad_own, grad_bottom = call(
        gather_kernel,
        [((EDGE, 2 * C), B16), ((CELLS, 2 * C), F32), ((EDGE, 2 * C), B16)],
        (grad_region, back_left, back_right),
    )
    from_below = lax.ppermute(grad_top, LAT, up)
    from_above = lax.ppermute(grad_bottom, LAT, down)

    mine, send, grad_mixed, grad_cross_att = call(
        mixed_kernel,
        half(ROWS_CELLS) + [((CELLS, C), F32), ((CELLS, C), B16)],
        (
            core, results, grad_own, from_above, from_below, grad_rows, local_weight,
            cross_weight,
        ),
        scratch=[pltpu.VMEM((2, ROWS_CELLS, 128), B16), pltpu.VMEM((CELLS, 2 * C), F32)],
        scalars=1,
        micros=3,
        loads=(5, 6, 7),
    )
    cells_mine, cells_partner = mine, lax.ppermute(send, "core", CORE_PAIRS)
    mine, send, grad_grid, grad_wire = call(
        cross_back_kernel,
        half(ROWS_LATE) + [((CELLS, C), F32), ((WIRE, F), B16)],
        (
            core, query, keyval, prob, grad_cross_att, grid, query_weight, sensor_weight,
            grad_mixed,
        ),
        scratch=[
            pltpu.VMEM((2, ROWS_LATE, 128), B16), pltpu.VMEM((SLOTS, LANES), F32),
            pltpu.VMEM((SLOTS, LANES), B16), pltpu.VMEM((CELLS, C), B16),
            pltpu.VMEM((SLOTS, 2 * C), B16), pltpu.VMEM((GROUPS, SLOTS, LANES), B16),
            pltpu.SemaphoreType.DMA((GROUPS,)),
        ],
        scalars=1,
        micros=9,
        loads=(1, 2, 5, 6, 7, 8),
        raw=(3,),
        megabytes=20,
    )
    (pair,) = call(
        sum_kernel, some(ROWS_CELLS, 1), (cells_mine, cells_partner), after=(grad_wire,)
    )
    parts = swapped_parts(pair.reshape(SIDE_COUNT, -1, 128), LAT)
    returned = lax.all_to_all(
        grad_wire.reshape(TILES, PITCH, F), ALL, split_axis=0, concat_axis=0, tiled=True
    ).reshape(WIRE, F)
    band = ROWS_CELLS // SIDE_COUNT
    thin = band // RING
    rows = ROWS_LATE // RING
    pieces = call(
        first_kernel, some(rows, RING),
        (spot("y"), mine, lax.ppermute(send, "core", CORE_PAIRS)), scalars=1,
    )
    late_parts = ring_sends("y", pieces)
    pieces = call(
        next_kernel, some(rows // RING, RING), (spot("x"), *late_parts),
        scratch=[pltpu.VMEM((rows, 128), F32)], scalars=1,
    )
    late_parts = ring_sends("x", pieces)
    (share,) = call(sum_kernel, some(rows // RING, 1), late_parts)
    bands = call(
        band_kernel, some(thin, RING), (spot("y"), parts),
        scratch=[pltpu.VMEM((band, 128), B16)], scalars=1, after=(share,),
    )
    late_parts = ring_sends(DEPTH, [share] * RING)
    (share,) = call(
        ordered_sum_kernel, some(rows // RING, 1), (spot(DEPTH), *late_parts),
        scratch=[pltpu.VMEM((RING, rows // RING, 128), F32)], scalars=1,
    )
    (inner,) = call(sum_kernel, some(thin, 1), ring_sends("y", bands), after=(share,))
    late_parts = ring_sends("x", [share] * RING)
    (share,) = call(joined_kernel, some(rows, 1), (spot("x"), *late_parts), scalars=1)
    (inner,) = call(
        sum_kernel, some(thin, 1), (inner, lax.ppermute(inner, "zhi", CORE_PAIRS)),
        after=(share,),
    )
    (grad_obs,) = call(
        return_kernel, [((OBS, F), B16)], (slot, returned), after=(inner,)
    )
    (spread,) = call(
        spread_kernel, [((SIDE_COUNT, band, 128), B16)],
        (spot("y"), *ring_sends("y", [inner] * RING)), scalars=1, after=(grad_obs,),
    )
    gathered = lax.all_to_all(spread, LAT, split_axis=0, concat_axis=0, tiled=True)
    late_parts = ring_sends("y", [share] * RING)
    (share,) = call(
        joined_kernel, some(ROWS_LATE, 1), (spot("y"), *late_parts), scalars=1, after=(spread,)
    )
    (gathered,) = call(
        hold_kernel, some(ROWS_CELLS, 1), (gathered.reshape(-1, 128),), after=(share,)
    )
    late = (share, lax.ppermute(share, "core", CORE_PAIRS))
    grad_merge, grad_local, grad_cross = call(
        unpack_cells_kernel,
        [((C, C), F32), ((C, 3 * C), F32), ((C, C), F32)],
        (core, gathered, lax.ppermute(gathered, "core", CORE_PAIRS)),
        scalars=1,
        micros=3,
    )
    grad_query_w, grad_sensor = call(
        unpack_late_kernel,
        [((C, C), F32), ((F, 2 * C), F32)],
        (core, *late),
        scalars=1,
        micros=2,
    )
    return (
        updated.reshape(TH, TW, C), grad_grid.reshape(TH, TW, C), grad_obs,
        grad_query_w, grad_sensor, grad_cross, grad_local, grad_merge,
    )


def solution(mesh):
    fine = Mesh(mesh.devices.reshape(2, 4, 4, 2, 2), ALL)
    in_specs = (
        P(LAT, LON, None), P(ALL, None), P(ALL, None), P(ALL), P(ALL),
        P(), P(), P(), P(), P(), P(LAT, LON, None),
    )
    out_specs = (P(LAT, LON, None), P(LAT, LON, None), P(ALL, None), P(), P(), P(), P(), P())
    return jax.shard_map(
        on_device, mesh=fine, in_specs=in_specs, out_specs=out_specs, check_vma=False
    )
```
